256 devices in a mesh: wide: 64 (over z, y, core), narrow: 4 (over x).
Axes of the slice: x: 4, y: 4, z: 8, core: 2. Of those that a mesh axis runs over, the one named last changes fastest.
Arguments:
- soil_state: bfloat16 [4, 5120, 256], P('narrow', 'wide'), may hold values from -0.3125 to 3, as said below
- directions: bfloat16 [4, 5120, 64, 128], P('narrow', 'wide'), may hold values from -6 to 6
- blocks: bfloat16 [4, 5120, 4096], P('narrow', 'wide'), may hold values from -0.75 to 0.75
- send_left: int32 [64], replicated, may hold values from 0 to 8, as said below
- send_right: int32 [64], replicated, may hold values from 0 to 8, as said below
- neighbours: int32 [4, 6, 4096], P('narrow', None, 'wide'), may hold values from -1 to 111, as said below
- face_blocks: bfloat16 [6, 64, 64], replicated, may hold values from -0.75 to 0.75
Outputs:
- second_product: bfloat16 [4, 4096, 64, 128], P('narrow', 'wide')
The draws below stay inside these ranges and needn't reach their ends.
Inputs may be any that keep to these rules, and one draw needn't show every extreme that they name: `send_left`: the first block sends nothing to the previous one; every other block sends at least one; some block sends exactly 8. `send_right`: the last block sends nothing to the next one; every other block sends at least one; some block sends exactly 8. `neighbours`: faces 0 to 3 are horizontal; positions 64 to 79 appear only outside the first wide block, 80 to 95 only outside the last. Face 4 points up and face 5 down: the element 8 slots before or after in the same block, or the matching element of the bottom or top layer of the sub-tile above or below; -1 at the surface and at the bottom of a column and at some horizontal catchment edges. `soil_state`: pressure heads lie in [-0.3125, -0.1], inverse air-entry values in [0.5, 1], pore indices in [1.4, 2.8], saturated conductivities in [0.3, 3]. Slots of a block beyond its live count hold values of the same ranges.
All inputs are finite; a program needn't handle non-finite values.
Results may differ from the reference program's by a relative error of at most 0.0064.
Values may be sent and summed in bfloat16 or wider, within the bound.
No kernel may reach another device: no remote copies, remote signals or barrier semaphores. Data moves between devices by JAX's collectives and lax.ppermute only.
A program may use at most 64 MiB of HBM per device.

```python
import math
import jax
import jax.numpy as jnp
from jax import lax

P_SIZE = 64
FACES = 6
NV = 128
E_BAL = 64
MIG = 8
RIM = 16
LAYER = 8
E_DEV = 80
COLS = 4
ELEMS = 4096
SLOTS = 5120
N_WIDE = 64


def draw_soil_state(key, part):
    subkeys = jax.random.split(key, 4)
    shape_one = (COLS, SLOTS, P_SIZE)
    shape_elem = (COLS, SLOTS, 1)
    pressure = jax.random.uniform(subkeys[0], shape_one, jnp.float32, -0.3125, -0.1)
    pore_elem = jax.random.uniform(subkeys[2], shape_elem, jnp.float32, 1.4, 2.8)
    entry_elem = jnp.exp(jax.random.uniform(subkeys[1], shape_elem, jnp.float32, math.log(0.5), math.log(1.0)))
    conduct_elem = jnp.exp(jax.random.uniform(subkeys[3], shape_elem, jnp.float32, math.log(0.3), math.log(3.0)))
    inverse_entry = jnp.broadcast_to(entry_elem, shape_one)
    pore_index = jnp.broadcast_to(pore_elem, shape_one)
    conduct_sat = jnp.broadcast_to(conduct_elem, shape_one)
    return jnp.concatenate([pressure, inverse_entry, pore_index, conduct_sat], -1).astype(jnp.bfloat16)


def draw_send_left(key, part):
    subkeys = jax.random.split(key, 2)
    amounts = jax.random.randint(subkeys[0], (N_WIDE,), 1, MIG + 1, jnp.int32)
    chosen = jax.random.randint(subkeys[1], (), 1, N_WIDE, jnp.int32)
    device_spot = jnp.arange(N_WIDE, dtype=jnp.int32)
    amounts = jnp.where(device_spot == chosen, MIG, amounts)
    return jnp.where(device_spot == 0, 0, amounts).astype(jnp.int32)


def draw_send_right(key, part):
    subkeys = jax.random.split(jax.random.fold_in(key, 7), 2)
    amounts = jax.random.randint(subkeys[0], (N_WIDE,), 1, MIG + 1, jnp.int32)
    chosen = jax.random.randint(subkeys[1], (), 0, N_WIDE - 1, jnp.int32)
    device_spot = jnp.arange(N_WIDE, dtype=jnp.int32)
    amounts = jnp.where(device_spot == chosen, MIG, amounts)
    return jnp.where(device_spot == N_WIDE - 1, 0, amounts).astype(jnp.int32)


def draw_neighbours(key, part):
    subkeys = jax.random.split(key, 3)
    layer_index = jnp.arange(COLS, dtype=jnp.int32)[:, None, None]
    element = jnp.arange(ELEMS, dtype=jnp.int32)[None, None, :]
    device_spot = element // E_BAL
    within = element % E_BAL
    shape_side = (COLS, 4, ELEMS)
    roll_value = jax.random.randint(subkeys[0], shape_side, 0, 100, jnp.int32)
    own_pick = jax.random.randint(subkeys[1], shape_side, 0, E_BAL, jnp.int32)
    rim_pick = jax.random.randint(subkeys[2], shape_side, 0, RIM, jnp.int32)
    sideways = jnp.where(roll_value >= 96, -1, own_pick)
    sideways = jnp.where((roll_value < 25) & (device_spot > 0), E_BAL + rim_pick, sideways)
    sideways = jnp.where((roll_value >= 25) & (roll_value < 50) & (device_spot < N_WIDE - 1), E_BAL + RIM + rim_pick, sideways)
    upward = jnp.where(within < LAYER, jnp.where(layer_index > 0, E_BAL + 2 * RIM + within, -1), within - LAYER)
    downward = jnp.where(within >= E_BAL - LAYER, jnp.where(layer_index < COLS - 1, E_BAL + 2 * RIM + LAYER + within - (E_BAL - LAYER), -1), within + LAYER)
    upward = jnp.broadcast_to(upward, (COLS, 1, ELEMS))
    downward = jnp.broadcast_to(downward, (COLS, 1, ELEMS))
    return jnp.concatenate([sideways, upward, downward], 1).astype(jnp.int32)


def steps_of(key, extent, cuts, low, high):
    factor_of = 1.0
    for position, blocks in cuts:
        steps = jax.random.uniform(jax.random.fold_in(jax.random.fold_in(key, 6), position), (blocks,), jnp.float32, low / len(cuts), high / len(cuts))
        factor_of = factor_of * jnp.repeat(jnp.exp(steps), extent[position] // blocks).reshape((-1,) + (1,) * (len(extent) - 1 - position))
    return factor_of


def centred(key, dims, deviation, limit, shards=(), kind=jnp.bfloat16):
    gain = steps_of(key, dims, shards, -0.22, 0.18) if shards else 1.0
    entries = jax.random.normal(key, dims, jnp.float32) * deviation * gain
    return jnp.minimum(jnp.maximum(entries, -limit), limit).astype(kind)


def setup_inputs(seed: int = 0) -> dict:
    streams_of = jax.random.split(jax.random.key(seed), 8)
    soil_state = draw_soil_state(jax.random.fold_in(streams_of[7], 71), 0)
    directions = centred(streams_of[1], (COLS, SLOTS, P_SIZE, NV), 1.0, 6.0, ((0, 4), (1, 64)))
    blocks = centred(streams_of[2], (COLS, SLOTS, P_SIZE * P_SIZE), P_SIZE ** -0.5, 0.75, ((0, 4), (1, 64)))
    send_left = draw_send_left(jax.random.fold_in(streams_of[7], 71), 0)
    send_right = draw_send_right(jax.random.fold_in(streams_of[7], 71), 0)
    neighbours = draw_neighbours(jax.random.fold_in(streams_of[7], 71), 0)
    face_blocks = centred(streams_of[6], (FACES, P_SIZE, P_SIZE), P_SIZE ** -0.5, 0.75)
    return {"soil_state": soil_state, "directions": directions, "blocks": blocks, "send_left": send_left, "send_right": send_right, "neighbours": neighbours, "face_blocks": face_blocks}


moisture_range = 0.4
time_step = 0.5

def closures(soil_rows):
    soil_float = soil_rows.astype(jnp.float32)
    pressure = soil_float[..., 0:P_SIZE]
    inverse_entry = soil_float[..., P_SIZE:2 * P_SIZE]
    pore_index = soil_float[..., 2 * P_SIZE:3 * P_SIZE]
    conduct_sat = soil_float[..., 3 * P_SIZE:4 * P_SIZE]
    exponent = 1.0 - 1.0 / pore_index
    log_scaled = jnp.log(-inverse_entry * pressure)
    power = jnp.exp(pore_index * log_scaled)
    log_denom = jnp.log1p(power)
    saturation = jnp.exp(-exponent * log_denom)
    ratio_log = pore_index * log_scaled - log_denom
    relative = jnp.sqrt(saturation) * jnp.square(1.0 - jnp.exp(exponent * ratio_log))
    capacity = moisture_range * inverse_entry * pore_index * exponent * jnp.exp((pore_index - 1.0) * log_scaled - (exponent + 1.0) * log_denom) / time_step
    return (capacity, conduct_sat * relative)

def source_rows(send_left, send_right):
    zero_one = jnp.zeros((1,), jnp.int32)
    arrive_left = jnp.concatenate([zero_one, send_right[:-1]])
    arrive_right = jnp.concatenate([send_left[1:], zero_one])
    live_rows = E_BAL + send_left + send_right - arrive_left - arrive_right
    element = jnp.arange(ELEMS, dtype=jnp.int32)
    target = element // E_BAL
    within = element % E_BAL
    before = jnp.maximum(target - 1, 0)
    after = jnp.minimum(target + 1, N_WIDE - 1)
    from_before = before * E_DEV + live_rows[before] - arrive_left[target] + within
    from_self = target * E_DEV + send_left[target] - arrive_left[target] + within
    from_after = after * E_DEV + within - (E_BAL - arrive_right[target])
    middle_or_after = jnp.where(within < E_BAL - arrive_right[target], from_self, from_after)
    return jnp.where(within < arrive_left[target], from_before, middle_or_after).astype(jnp.int32)

def neighbour_rows(neighbours):
    layer_index = jnp.arange(COLS, dtype=jnp.int32)[:, None, None]
    element = jnp.arange(ELEMS, dtype=jnp.int32)[None, None, :]
    target = element // E_BAL
    own_base = layer_index * ELEMS + target * E_BAL
    picked = neighbours
    rows = own_base + ELEMS + (picked - E_BAL - 2 * RIM - LAYER)
    rows = jnp.where(picked < E_BAL + 2 * RIM + LAYER, own_base - ELEMS + E_BAL - LAYER + (picked - E_BAL - 2 * RIM), rows)
    rows = jnp.where(picked < E_BAL + 2 * RIM, own_base + E_BAL + (picked - E_BAL - RIM), rows)
    rows = jnp.where(picked < E_BAL + RIM, own_base - RIM + (picked - E_BAL), rows)
    rows = jnp.where(picked < E_BAL, own_base + picked, rows)
    rows = jnp.where(picked < 0, COLS * ELEMS, rows)
    return jnp.transpose(rows, (0, 2, 1)).reshape(COLS * ELEMS, FACES).astype(jnp.int32)

def reference(soil_state, directions, blocks, send_left, send_right, neighbours, face_blocks):
    total = COLS * ELEMS
    groups = total // E_BAL
    source = source_rows(send_left, send_right)
    picked = (jnp.arange(COLS, dtype=jnp.int32)[:, None] * SLOTS + source[None, :]).reshape(total).astype(jnp.int32)
    soil_flat = soil_state.reshape(COLS * SLOTS, 4 * P_SIZE)
    direction_flat = directions.reshape(COLS * SLOTS, P_SIZE, NV)
    block_flat = blocks.reshape(COLS * SLOTS, P_SIZE * P_SIZE)
    capacity, weight = closures(soil_flat[picked])
    faces_float = face_blocks.astype(jnp.float32)
    rows_all = neighbour_rows(neighbours)
    group_ids = jnp.arange(groups, dtype=jnp.int32)

    def first_vectors(start):
        return direction_flat[lax.dynamic_slice_in_dim(picked, start, E_BAL, 0)]

    def weigh_all(fetch):

        def one_group(group):
            start = group * E_BAL
            scale = lax.dynamic_slice_in_dim(weight, start, E_BAL, 0)
            return (scale[:, :, None] * fetch(start).astype(jnp.float32)).astype(jnp.bfloat16)
        return lax.map(one_group, group_ids).reshape(total, P_SIZE, NV)

    def jacobian(fetch, weighted):

        def one_group(group):
            start = group * E_BAL
            vectors = fetch(start).astype(jnp.float32)
            own_weighted = lax.dynamic_slice_in_dim(weighted, start, E_BAL, 0).astype(jnp.float32)
            cap_rows = lax.dynamic_slice_in_dim(capacity, start, E_BAL, 0)
            block_rows = block_flat[lax.dynamic_slice_in_dim(picked, start, E_BAL, 0)].reshape(E_BAL, P_SIZE, P_SIZE).astype(jnp.float32)
            result = cap_rows[:, :, None] * vectors + jnp.einsum('eij,ejv->eiv', block_rows, own_weighted)
            near_rows = lax.dynamic_slice_in_dim(rows_all, start, E_BAL, 0)
            for face_index in range(FACES):
                nearby = jnp.take(weighted, near_rows[:, face_index], axis=0, mode='fill', fill_value=0.0)
                result = result - jnp.einsum('ij,ejv->eiv', faces_float[face_index], nearby.astype(jnp.float32))
            return result.astype(jnp.bfloat16)
        return lax.map(one_group, group_ids).reshape(total, P_SIZE, NV)
    weighted = weigh_all(first_vectors)
    first_product = jacobian(first_vectors, weighted)

    def next_vectors(start):
        return lax.dynamic_slice_in_dim(first_product, start, E_BAL, 0)
    weighted_next = weigh_all(next_vectors)
    second_product = jacobian(next_vectors, weighted_next)
    return second_product.reshape(COLS, ELEMS, P_SIZE, NV)
```

```python
import jax
import jax.numpy as jnp
from jax import lax
from jax.experimental import pallas as pl
from jax.experimental.pallas import tpu as pltpu
from jax.sharding import PartitionSpec as P

P_SIZE = 64
FACES = 6
NV = 128
E_BAL = 64
MIG = 8
RIM = 16
LAYER = 8
E_DEV = 80
N_WIDE = 64
COLS = 4
HALF = P_SIZE // 2
ABOVE = E_BAL + 2 * RIM
BELOW = ABOVE + LAYER
MISSING = BELOW + LAYER

DIR_AT = RIM * P_SIZE
BLK_AT = DIR_AT + MIG * P_SIZE
SOIL_AT = BLK_AT + MIG * HALF
MESSAGE = SOIL_AT + 2 * MIG

moisture_range = 0.4
time_step = 0.5

F32 = jnp.float32
BF16 = jnp.bfloat16


def closures(pressure, inverse_entry, pore_index, conduct_sat):
    exponent = 1.0 - 1.0 / pore_index
    log_scaled = jnp.log(-inverse_entry * pressure)
    power = jnp.exp(pore_index * log_scaled)
    log_denom = jnp.log1p(power)
    saturation = jnp.exp(-exponent * log_denom)
    ratio_log = pore_index * log_scaled - log_denom
    relative = jnp.sqrt(saturation) * jnp.square(1.0 - jnp.exp(exponent * ratio_log))
    capacity = (
        moisture_range
        * inverse_entry
        * pore_index
        * exponent
        * jnp.exp((pore_index - 1.0) * log_scaled - (exponent + 1.0) * log_denom)
        / time_step
    )
    return capacity, conduct_sat * relative


def closures_by_column(soil_rows):
    cols = [jnp.transpose(soil_rows[k * NV : (k + 1) * NV]) for k in range(2)]
    fields = [cols[i // 2][i % 2 * P_SIZE : (i % 2 + 1) * P_SIZE] for i in range(4)]
    return closures(*fields)


def counts(send_left, send_right):
    t = lax.axis_index("wide")
    before = lax.rem(t + N_WIDE - 1, N_WIDE)
    after = lax.rem(t + 1, N_WIDE)
    mine_left = send_left[t]
    mine_right = send_right[t]
    arrive_left = jnp.where(t > 0, send_right[before], 0)
    arrive_right = jnp.where(t < N_WIDE - 1, send_left[after], 0)
    live = E_BAL + mine_left + mine_right - arrive_left - arrive_right
    return mine_left, mine_right, arrive_left, arrive_right, live


def rows(index, size=P_SIZE, base=0):
    if isinstance(index, int):
        return pl.ds(base + index * size, size)
    return pl.ds(pl.multiple_of(base + index * size, 16), size)


def wide_column(columns, lane):
    return jnp.broadcast_to(columns[:, lane : lane + 1], (P_SIZE, NV))


def lane_is(p):
    return (lax.broadcasted_iota(jnp.int32, (1, NV), 1) >= P_SIZE) == bool(p)


def prepare_kernel(sl, sr, soil, dirs, blocks, to_right, to_left, cap_out, wt_out, soil_f, blk_f, wb):
    mine_left, mine_right, arrive_left, arrive_right, live = counts(sl, sr)
    for k in range(2):
        soil_f[k * NV : k * NV + E_DEV, :] = soil[:, k * NV : (k + 1) * NV].astype(F32)
        soil_f[k * NV + E_DEV : (k + 1) * NV, :] = jnp.full((NV - E_DEV, NV), 1.0, F32)
    capacity, weight = closures_by_column(soil_f[...])
    cap_out[...] = capacity
    wt_out[...] = weight
    for s in range(E_DEV):
        if s < 24 or s >= 40:
            wb[rows(s), :] = wide_column(weight, s)
    tail = live - MIG
    group = jnp.minimum(lax.div(tail, 16) * 16, E_DEV - 32)
    for g in range(3):
        for c in range(HALF):
            lanes = slice(c * NV, (c + 1) * NV)
            if g == 0:
                x = blocks[0:16, lanes]
            else:
                x = blocks[pl.ds(pl.multiple_of(group + 16 * (g - 1), 16), 16), lanes]
            blk_f[pl.ds(g * 16 * HALF + c, 16, stride=HALF), :] = x.astype(F32)
    middle = mine_left - arrive_left
    for i in range(RIM):
        s = middle + E_BAL - RIM + i
        to_right[rows(i), :] = (wb[rows(s), :] * dirs[rows(s), :].astype(F32)).astype(BF16)
        s = jnp.maximum(middle + i, 0)
        to_left[rows(i), :] = (wb[rows(s), :] * dirs[rows(s), :].astype(F32)).astype(BF16)
    to_right[pl.ds(DIR_AT, MIG * P_SIZE), :] = dirs[pl.ds(pl.multiple_of(tail * P_SIZE, P_SIZE), MIG * P_SIZE), :]
    to_left[pl.ds(DIR_AT, MIG * P_SIZE), :] = dirs[0 : MIG * P_SIZE, :]
    at = pl.multiple_of((16 + tail - group) * HALF, HALF)
    to_right[pl.ds(BLK_AT, MIG * HALF), :] = blk_f[pl.ds(at, MIG * HALF), :].astype(BF16)
    to_left[pl.ds(BLK_AT, MIG * HALF), :] = blk_f[0 : MIG * HALF, :].astype(BF16)
    for out, first in ((to_right, tail), (to_left, 0)):
        both = jnp.concatenate([soil_f[pl.ds(k * NV + first, MIG), :] for k in range(2)], 0)
        out[pl.ds(SOIL_AT, 2 * MIG), :] = both.astype(BF16)


def own_kernel(wt, dirs, blocks, weighted, matrices, blk_f):
    weight = wt[...]
    for s in range(E_DEV):
        weighted[rows(s), :] = (wide_column(weight, s) * dirs[rows(s), :].astype(F32)).astype(BF16)
    for g in range(E_DEV // 16):
        for c in range(HALF):
            x = blocks[g * 16 : (g + 1) * 16, c * NV : (c + 1) * NV].astype(F32)
            for p in range(2):
                blk_f[pl.ds(2 * c + p, 16, stride=P_SIZE), :] = jnp.where(lane_is(p), x, 0.0)
        matrices[g * 16 * P_SIZE : (g + 1) * 16 * P_SIZE, :] = blk_f[...].astype(BF16)


def arrive_kernel(sl, sr, cap_own, wt_own, soil_l, soil_r, dir_l, dir_r, own, to_above, to_below, moved, cap_out, wt_out, soil_f):
    mine_left, mine_right, arrive_left, arrive_right, live = counts(sl, sr)
    soil_f[...] = jnp.full((2 * NV, NV), 1.0, F32)
    for side, ref in enumerate((soil_l, soil_r)):
        x = ref[...].astype(F32)
        for k in range(2):
            soil_f[k * NV + side * MIG : k * NV + (side + 1) * MIG, :] = x[k * MIG : (k + 1) * MIG]
    capacity, weight = closures_by_column(soil_f[...])
    lane = lax.broadcasted_iota(jnp.int32, (P_SIZE, NV), 1)
    for out, mine, theirs in ((cap_out, cap_own, capacity), (wt_out, wt_own, weight)):
        middle = pltpu.roll(mine[...], lax.rem(arrive_left - mine_left + NV, NV), 1)
        left = pltpu.roll(theirs, lax.rem(arrive_left - MIG + NV, NV), 1)
        right = pltpu.roll(theirs, E_BAL - arrive_right - MIG, 1)
        out[...] = jnp.where(lane < arrive_left, left, jnp.where(lane < E_BAL - arrive_right, middle, right))
    for i in range(MIG):
        moved[rows(i), :] = (wide_column(weight, i) * dir_l[rows(i), :].astype(F32)).astype(BF16)
        moved[rows(MIG + i), :] = (wide_column(weight, MIG + i) * dir_r[rows(i), :].astype(F32)).astype(BF16)
    shift = mine_left - arrive_left
    for i in range(LAYER):
        here = own[rows(jnp.maximum(shift + i, 0)), :].astype(F32)
        came = moved[rows(jnp.minimum(MIG - arrive_left + i, MIG - 1)), :].astype(F32)
        to_above[rows(i), :] = jnp.where(i < arrive_left, came, here).astype(BF16)
        w = E_BAL - LAYER + i
        here = own[rows(shift + w), :].astype(F32)
        came = moved[rows(jnp.maximum(w - E_BAL + arrive_right, 0) + MIG), :].astype(F32)
        to_below[rows(i), :] = jnp.where(w >= E_BAL - arrive_right, came, here).astype(BF16)


def first_kernel(
    sl, sr, nbr, cap, wt, faces, dirs, own, matrices, moved, above, below, from_left, from_right,
    near, blk_out, partial, first, nxt, blk_f,
):
    mine_left, mine_right, arrive_left, arrive_right, live = counts(sl, sr)
    shift = mine_left - arrive_left
    for w in range(E_BAL):
        if w < LAYER:
            near[rows(w), :] = above[rows(w), :]
        elif w >= E_BAL - LAYER:
            near[rows(w), :] = below[rows(w - E_BAL + LAYER), :]
        else:
            near[rows(w), :] = own[rows(shift + w), :]
    for i in range(RIM):
        near[rows(E_BAL + i), :] = from_left[rows(i), :]
        near[rows(E_BAL + RIM + i), :] = from_right[rows(i), :]
    for i in range(MIG):

        @pl.when(i < mine_left)
        def _():
            near[rows(E_BAL + RIM - mine_left + i), :] = own[rows(i), :]

        @pl.when(i < mine_right)
        def _():
            near[rows(E_BAL + RIM + i), :] = own[rows(live - mine_right + i), :]

    near[rows(ABOVE), :] = jnp.zeros((P_SIZE, NV), BF16)

    for w in range(E_BAL):
        blk_out[rows(w), :] = matrices[rows(jnp.maximum(shift + w, 0)), :]
    for i in range(MIG):

        @pl.when(i < arrive_left)
        def _():
            x = from_left[rows(MIG - arrive_left + i, HALF, BLK_AT), :].astype(F32)
            for p in range(2):
                blk_f[pl.ds(p, HALF, stride=2), :] = jnp.where(lane_is(p), x, 0.0)
            blk_out[rows(i), :] = blk_f[...].astype(BF16)

        @pl.when(i < arrive_right)
        def _():
            x = from_right[rows(i, HALF, BLK_AT), :].astype(F32)
            for p in range(2):
                blk_f[pl.ds(p, HALF, stride=2), :] = jnp.where(lane_is(p), x, 0.0)
            blk_out[rows(E_BAL - arrive_right + i), :] = blk_f[...].astype(BF16)

    capacity = cap[...]
    weight = wt[...]
    face_rows = faces[...]
    for w in range(E_BAL):
        vector = dirs[rows(jnp.maximum(shift + w, 0)), :].astype(F32)
        if w < MIG:
            came = from_left[rows(jnp.minimum(MIG - arrive_left + w, MIG - 1), base=DIR_AT), :].astype(F32)
            vector = jnp.where(w < arrive_left, came, vector)
        elif w >= E_BAL - MIG:
            came = from_right[rows(jnp.maximum(w - E_BAL + arrive_right, 0), base=DIR_AT), :].astype(F32)
            vector = jnp.where(w >= E_BAL - arrive_right, came, vector)
        result = wide_column(capacity, w) * vector + product(near, nbr, blk_out, face_rows, w, ABOVE, ABOVE)
        if LAYER <= w < E_BAL - LAYER:
            rounded = result.astype(BF16)
            first[rows(w - LAYER), :] = rounded
            nxt[rows(w - LAYER), :] = (wide_column(weight, w) * rounded.astype(F32)).astype(BF16)
        else:
            partial[rows(w if w < LAYER else w - E_BAL + 2 * LAYER), :] = result


def product(near, nbr, matrices, face_rows, w, limit, missing):
    mine = near[rows(w), :]
    parts = [mine, mine]
    for k in range(FACES):
        b = nbr[k, w]
        b = jnp.where((b < 0) | (b >= limit), missing, b)
        parts.append(near[rows(b), :])
    lhs = jnp.concatenate([matrices[rows(w), :], face_rows], 1)
    return jnp.dot(lhs, jnp.concatenate(parts, 0), preferred_element_type=F32)


def ends_kernel(nbr, wt, faces, partial, from_above, from_below, nxt, first, to_right, to_left, to_above, to_below):
    weight = wt[...]
    for i in range(2 * LAYER):
        top = i < LAYER
        w = i if top else E_BAL - 2 * LAYER + i
        k = 4 if top else 5
        came = from_above if top else from_below
        b = nbr[k, w]
        inside = b - (ABOVE if top else BELOW)
        there = (inside >= 0) & (inside < LAYER)
        row = came[rows(jnp.clip(inside, 0, LAYER - 1)), :]
        update = jnp.dot(faces[:, k * P_SIZE : (k + 1) * P_SIZE], row, preferred_element_type=F32)
        rounded = (partial[rows(i), :] + jnp.where(there, update, 0.0)).astype(BF16)
        first[rows(i), :] = rounded
        onward = (wide_column(weight, w) * rounded.astype(F32)).astype(BF16)
        if top:
            to_left[rows(i), :] = onward
            to_above[rows(i), :] = onward
        else:
            to_right[rows(i), :] = onward
            to_below[rows(i - LAYER), :] = onward
    span = LAYER * P_SIZE
    to_left[span : 2 * span, :] = nxt[0:span, :]
    to_right[0:span, :] = nxt[(E_BAL - 3 * LAYER) * P_SIZE : (E_BAL - 2 * LAYER) * P_SIZE, :]


def second_kernel(
    nbr, cap, faces, matrices, mid, ends, nxt, sent_left, sent_right, from_left, from_right, from_above, from_below,
    out, near,
):
    near[0 : RIM * P_SIZE, :] = sent_left[...]
    near[RIM * P_SIZE : (E_BAL - RIM) * P_SIZE, :] = nxt[LAYER * P_SIZE : (E_BAL - RIM - LAYER) * P_SIZE, :]
    near[(E_BAL - RIM) * P_SIZE : E_BAL * P_SIZE, :] = sent_right[...]
    near[E_BAL * P_SIZE : (E_BAL + RIM) * P_SIZE, :] = from_left[...]
    near[(E_BAL + RIM) * P_SIZE : ABOVE * P_SIZE, :] = from_right[...]
    near[ABOVE * P_SIZE : BELOW * P_SIZE, :] = from_above[...]
    near[BELOW * P_SIZE : MISSING * P_SIZE, :] = from_below[...]
    near[rows(MISSING), :] = jnp.zeros((P_SIZE, NV), BF16)
    capacity = cap[...]
    face_rows = faces[...]
    for w in range(E_BAL):
        if w < LAYER:
            vector = ends[rows(w), :]
        elif w >= E_BAL - LAYER:
            vector = ends[rows(w - E_BAL + 2 * LAYER), :]
        else:
            vector = mid[rows(w - LAYER), :]
        result = wide_column(capacity, w) * vector.astype(F32) + product(
            near, nbr, matrices, face_rows, w, MISSING, MISSING
        )
        out[rows(w), :] = result.astype(BF16)


def smem():
    return pl.BlockSpec(memory_space=pltpu.SMEM)


def vmem():
    return pl.BlockSpec(memory_space=pltpu.VMEM)


def shape(n, kind=BF16):
    return jax.ShapeDtypeStruct((n, NV), kind)


def call(kernel, name, scalars, arrays, outs, scratch=(), flops=0, moved=0):
    return pl.pallas_call(
        kernel,
        out_shape=outs,
        in_specs=[smem()] * len(scalars) + [vmem()] * len(arrays),
        out_specs=[vmem()] * len(outs),
        scratch_shapes=list(scratch),
        compiler_params=pltpu.CompilerParams(vmem_limit_bytes=40 * 2**20),
        cost_estimate=pl.CostEstimate(flops=flops, bytes_accessed=moved, transcendentals=0),
        name=name,
    )(*scalars, *arrays)


def shifted(value, axis, by):
    peers = lax.axis_size(axis)
    return lax.ppermute(value, axis, [(i, (i + by) % peers) for i in range(peers)])


def per_device(soil_state, directions, blocks, send_left, send_right, neighbours, face_blocks):
    soil = soil_state[0]
    dirs = directions.reshape(E_DEV * P_SIZE, NV)
    rows_of = blocks[0]
    nbr = neighbours[0]
    faces = -jnp.swapaxes(face_blocks, 0, 1).reshape(P_SIZE, FACES * P_SIZE)
    column = shape(P_SIZE, F32)

    to_right, to_left, cap_own, wt_own = call(
        prepare_kernel, "prepare", (send_left, send_right), (soil, dirs, rows_of),
        (shape(MESSAGE), shape(MESSAGE), column, column),
        (pltpu.VMEM((2 * NV, NV), F32), pltpu.VMEM((48 * HALF, NV), F32), pltpu.VMEM((E_DEV * P_SIZE, NV), F32)),
    )
    from_left = shifted(to_right, "wide", 1)
    from_right = shifted(to_left, "wide", -1)

    own, matrices = call(
        own_kernel, "own", (), (wt_own, dirs, rows_of),
        (shape(E_DEV * P_SIZE), shape(E_DEV * P_SIZE)),
        (pltpu.VMEM((16 * P_SIZE, NV), F32),),
        flops=10**9, moved=6 * 2**20,
    )

    soil_l, soil_r = from_left[SOIL_AT:], from_right[SOIL_AT:]
    dir_l, dir_r = from_left[DIR_AT:BLK_AT], from_right[DIR_AT:BLK_AT]
    above, below, moved, cap, wt = call(
        arrive_kernel, "arrive", (send_left, send_right), (cap_own, wt_own, soil_l, soil_r, dir_l, dir_r, own),
        (shape(LAYER * P_SIZE), shape(LAYER * P_SIZE), shape(2 * MIG * P_SIZE), column, column),
        (pltpu.VMEM((2 * NV, NV), F32),),
    )
    from_below = shifted(above, "narrow", -1)
    from_above = shifted(below, "narrow", 1)

    near, blk, partial, first, nxt = call(
        first_kernel, "first", (send_left, send_right, nbr),
        (cap, wt, faces, dirs, own, matrices, moved, above, below, from_left, from_right),
        (
            shape((ABOVE + 1) * P_SIZE), shape(E_BAL * P_SIZE), shape(2 * LAYER * P_SIZE, F32),
            shape((E_BAL - 2 * LAYER) * P_SIZE), shape((E_BAL - 2 * LAYER) * P_SIZE),
        ),
        (pltpu.VMEM((P_SIZE, NV), F32),),
        flops=2 * 10**9, moved=8 * 2**20,
    )
    ends, go_right, go_left, go_above, go_below = call(
        ends_kernel, "ends", (nbr,), (wt, faces, partial, from_above, from_below, nxt),
        (
            shape(2 * LAYER * P_SIZE), shape(RIM * P_SIZE), shape(RIM * P_SIZE),
            shape(LAYER * P_SIZE), shape(LAYER * P_SIZE),
        ),
    )
    came_below = shifted(go_above, "narrow", -1)
    came_above = shifted(go_below, "narrow", 1)
    came_left = shifted(go_right, "wide", 1)
    came_right = shifted(go_left, "wide", -1)
    (out,) = call(
        second_kernel, "second", (nbr,),
        (cap, faces, blk, first, ends, nxt, go_left, go_right, came_left, came_right, came_above, came_below),
        (shape(E_BAL * P_SIZE),),
        (pltpu.VMEM(((MISSING + 1) * P_SIZE, NV), BF16),),
        flops=10**9, moved=6 * 2**20,
    )
    return out.reshape(1, E_BAL, P_SIZE, NV)


def solution(mesh):
    in_specs = (
        P("narrow", "wide", None),
        P("narrow", "wide", None, None),
        P("narrow", "wide", None),
        P(),
        P(),
        P("narrow", None, "wide"),
        P(),
    )
    out_specs = P("narrow", "wide", None, None)
    return jax.shard_map(
        per_device, mesh=mesh, in_specs=in_specs, out_specs=out_specs, check_vma=False
    )
```

```python
import jax
import jax.numpy as jnp
from jax import lax
from jax.experimental import pallas as pl
from jax.experimental.pallas import tpu as pltpu
from jax.sharding import PartitionSpec as P

P_SIZE = 64
FACES = 6
NV = 128
E_BAL = 64
MIG = 8
RIM = 16
LAYER = 8
E_DEV = 80
N_WIDE = 64
COLS = 4
HALF = P_SIZE // 2
ABOVE = E_BAL + 2 * RIM
BELOW = ABOVE + LAYER
MISSING = BELOW + LAYER

DIR_AT = RIM * P_SIZE
BLK_AT = DIR_AT + MIG * P_SIZE
SOIL_AT = BLK_AT + MIG * HALF
MESSAGE = SOIL_AT + 2 * MIG

moisture_range = 0.4
time_step = 0.5

F32 = jnp.float32
BF16 = jnp.bfloat16


def closures(pressure, inverse_entry, pore_index, conduct_sat):
    exponent = 1.0 - 1.0 / pore_index
    log_scaled = jnp.log(-inverse_entry * pressure)
    power = jnp.exp(pore_index * log_scaled)
    log_denom = jnp.log1p(power)
    saturation = jnp.exp(-exponent * log_denom)
    ratio_log = pore_index * log_scaled - log_denom
    relative = jnp.sqrt(saturation) * jnp.square(1.0 - jnp.exp(exponent * ratio_log))
    capacity = (
        moisture_range
        * inverse_entry
        * pore_index
        * exponent
        * jnp.exp((pore_index - 1.0) * log_scaled - (exponent + 1.0) * log_denom)
        / time_step
    )
    return capacity, conduct_sat * relative


def closures_by_column(soil_rows):
    cols = [jnp.transpose(soil_rows[k * NV : (k + 1) * NV]) for k in range(2)]
    fields = [cols[i // 2][i % 2 * P_SIZE : (i % 2 + 1) * P_SIZE] for i in range(4)]
    return closures(*fields)


def counts(send_left, send_right):
    t = lax.axis_index("wide")
    before = lax.rem(t + N_WIDE - 1, N_WIDE)
    after = lax.rem(t + 1, N_WIDE)
    mine_left = send_left[t]
    mine_right = send_right[t]
    arrive_left = jnp.where(t > 0, send_right[before], 0)
    arrive_right = jnp.where(t < N_WIDE - 1, send_left[after], 0)
    return mine_left, mine_right, arrive_left, arrive_right


PARITY = 4


def sides(cnt):
    return 1 - cnt[PARITY], cnt[PARITY]


def part(side, size):
    return pl.ds(pl.multiple_of(side * size, size if size % 16 == 0 else 16), size)


def moves(cnt):
    mine_left, mine_right, arrive_left, arrive_right = (cnt[i] for i in range(4))
    live = E_BAL + mine_left + mine_right - arrive_left - arrive_right
    return mine_left, mine_right, arrive_left, arrive_right, live


def rows(index, size=P_SIZE, base=0):
    if isinstance(index, int):
        return pl.ds(base + index * size, size)
    return pl.ds(pl.multiple_of(base + index * size, 16), size)


def wide_column(columns, lane):
    return jnp.broadcast_to(columns[:, lane : lane + 1], (P_SIZE, NV))


def lane_is(p):
    return (lax.broadcasted_iota(jnp.int32, (1, NV), 1) >= P_SIZE) == bool(p)


HEAD = MIG + RIM
TAIL = E_DEV - 40
BLK_TAIL = E_DEV - 32


def prepare_kernel(
    sl, sr, nbr, soil, dirs, blocks, to_pair, to_other, cap_out, wt_out, cnt, nbr_out,
    sl_s, sr_s, soil_b, soil_f, dir_head, dir_tail, blk_head, blk_tail, blk_f, message, sems,
):
    to_left = message.at[pl.ds(0, MESSAGE)]
    to_right = message.at[pl.ds(MESSAGE, MESSAGE)]
    copies = [
        pltpu.make_async_copy(source, target, sems.at[i])
        for i, (source, target) in enumerate((
            (soil, soil_b),
            (sl, sl_s),
            (sr, sr_s),
            (dirs.at[pl.ds(0, HEAD * P_SIZE)], dir_head),
            (dirs.at[pl.ds((E_DEV - TAIL) * P_SIZE, TAIL * P_SIZE)], dir_tail),
            (blocks.at[pl.ds(0, 16)], blk_head),
            (blocks.at[pl.ds(E_DEV - BLK_TAIL, BLK_TAIL)], blk_tail),
            (nbr, nbr_out),
        ))
    ]
    for copy in copies:
        copy.start()
    for k in range(2):
        soil_f[k * NV + E_DEV : (k + 1) * NV, :] = jnp.full((NV - E_DEV, NV), 1.0, F32)
    copies[0].wait()
    for k in range(2):
        soil_f[k * NV : k * NV + E_DEV, :] = soil_b[:, k * NV : (k + 1) * NV].astype(F32)
    capacity, weight = closures_by_column(soil_f[...])
    wt_out[...] = weight
    cap_out[...] = capacity
    copies[1].wait()
    copies[2].wait()
    for i, n in enumerate(counts(sl_s, sr_s)):
        cnt[i] = n
    cnt[PARITY] = lax.rem(lax.axis_index("wide"), 2)
    mine_left, mine_right, arrive_left, arrive_right, live = moves(cnt)
    middle = mine_left - arrive_left
    tail = live - MIG
    here = pltpu.roll(weight, lax.rem(NV - middle, NV), 1)
    copies[3].wait()
    copies[4].wait()
    for i in range(RIM):
        s = middle + E_BAL - RIM + i - (E_DEV - TAIL)
        to_right[rows(i), :] = (wide_column(here, E_BAL - RIM + i) * dir_tail[rows(s), :].astype(F32)).astype(BF16)
        s = jnp.maximum(middle + i, 0)
        to_left[rows(i), :] = (wide_column(here, i) * dir_head[rows(s), :].astype(F32)).astype(BF16)
    at = pl.multiple_of((tail - (E_DEV - TAIL)) * P_SIZE, P_SIZE)
    to_right[pl.ds(DIR_AT, MIG * P_SIZE), :] = dir_tail[pl.ds(at, MIG * P_SIZE), :]
    to_left[pl.ds(DIR_AT, MIG * P_SIZE), :] = dir_head[0 : MIG * P_SIZE, :]
    for out, first in ((to_right, tail), (to_left, 0)):
        both = jnp.concatenate([soil_f[pl.ds(k * NV + first, MIG), :] for k in range(2)], 0)
        out[pl.ds(SOIL_AT, 2 * MIG), :] = both.astype(BF16)
    copies[5].wait()
    copies[6].wait()
    start = E_DEV - BLK_TAIL
    group = jnp.minimum(lax.div(tail - start, 16) * 16, BLK_TAIL - 32)
    for g in range(3):
        for c in range(HALF):
            lanes = slice(c * NV, (c + 1) * NV)
            if g == 0:
                x = blk_head[:, lanes]
            else:
                x = blk_tail[pl.ds(pl.multiple_of(group + 16 * (g - 1), 16), 16), lanes]
            blk_f[pl.ds(g * 16 * HALF + c, 16, stride=HALF), :] = x.astype(F32)
    at = pl.multiple_of((16 + tail - start - group) * HALF, HALF)
    to_right[pl.ds(BLK_AT, MIG * HALF), :] = blk_f[pl.ds(at, MIG * HALF), :].astype(BF16)
    to_left[pl.ds(BLK_AT, MIG * HALF), :] = blk_f[0 : MIG * HALF, :].astype(BF16)
    for out, side in zip((to_pair, to_other), sides(cnt)):
        out[...] = message[part(side, MESSAGE), :]
    copies[7].wait()


def own_kernel(wt, dirs, blocks, face_blocks, weighted, matrices, faces, blk_f):
    for k in range(FACES):
        faces[:, k * P_SIZE : (k + 1) * P_SIZE] = -face_blocks[k]
    weight = wt[...]
    for s in range(E_DEV):
        weighted[rows(s), :] = (wide_column(weight, s) * dirs[rows(s), :].astype(F32)).astype(BF16)
    for g in range(E_DEV // 16):
        for c in range(HALF):
            x = blocks[g * 16 : (g + 1) * 16, c * NV : (c + 1) * NV].astype(F32)
            for p in range(2):
                blk_f[pl.ds(2 * c + p, 16, stride=P_SIZE), :] = jnp.where(lane_is(p), x, 0.0)
        matrices[g * 16 * P_SIZE : (g + 1) * 16 * P_SIZE, :] = blk_f[...].astype(BF16)


ARRIVED = MESSAGE - DIR_AT
BLK_IN = BLK_AT - DIR_AT
SOIL_IN = SOIL_AT - DIR_AT


def arrive_kernel(cnt, cap_own, wt_own, pair, other, own, to_above, to_below, came, cap_out, wt_out, moved, soil_f):
    mine_left, mine_right, arrive_left, arrive_right, live = moves(cnt)
    for ref, side in zip((pair, other), sides(cnt)):
        came[part(side, ARRIVED), :] = ref[DIR_AT:, :]
    soil_f[...] = jnp.full((2 * NV, NV), 1.0, F32)
    for side in range(2):
        x = came[pl.ds(side * ARRIVED + SOIL_IN, 2 * MIG), :].astype(F32)
        for k in range(2):
            soil_f[k * NV + side * MIG : k * NV + (side + 1) * MIG, :] = x[k * MIG : (k + 1) * MIG]
    capacity, weight = closures_by_column(soil_f[...])
    lane = lax.broadcasted_iota(jnp.int32, (P_SIZE, NV), 1)
    for out, mine, theirs in ((cap_out, cap_own, capacity), (wt_out, wt_own, weight)):
        middle = pltpu.roll(mine[...], lax.rem(arrive_left - mine_left + NV, NV), 1)
        left = pltpu.roll(theirs, lax.rem(arrive_left - MIG + NV, NV), 1)
        right = pltpu.roll(theirs, E_BAL - arrive_right - MIG, 1)
        out[...] = jnp.where(lane < arrive_left, left, jnp.where(lane < E_BAL - arrive_right, middle, right))
    for i in range(2 * MIG):
        raw = came[rows(i % MIG, base=i // MIG * ARRIVED), :]
        moved[rows(i), :] = (wide_column(weight, i) * raw.astype(F32)).astype(BF16)
    shift = mine_left - arrive_left
    for i in range(LAYER):
        here = own[rows(jnp.maximum(shift + i, 0)), :].astype(F32)
        came = moved[rows(jnp.minimum(MIG - arrive_left + i, MIG - 1)), :].astype(F32)
        to_above[rows(i), :] = jnp.where(i < arrive_left, came, here).astype(BF16)
        w = E_BAL - LAYER + i
        here = own[rows(shift + w), :].astype(F32)
        came = moved[rows(jnp.maximum(w - E_BAL + arrive_right, 0) + MIG), :].astype(F32)
        to_below[rows(i), :] = jnp.where(w >= E_BAL - arrive_right, came, here).astype(BF16)


def first_kernel(
    cnt, nbr, cap, wt, faces, dirs, own, matrices, came, above, below, pair, other,
    blk_out, partial, first, nxt, near, blk_f,
):
    mine_left, mine_right, arrive_left, arrive_right, live = moves(cnt)
    shift = mine_left - arrive_left
    for w in range(E_BAL):
        if w < LAYER:
            near[rows(w), :] = above[rows(w), :]
        elif w >= E_BAL - LAYER:
            near[rows(w), :] = below[rows(w - E_BAL + LAYER), :]
        else:
            near[rows(w), :] = own[rows(shift + w), :]
    for ref, side in zip((pair, other), sides(cnt)):
        at = pl.multiple_of((E_BAL + side * RIM) * P_SIZE, P_SIZE)
        near[pl.ds(at, RIM * P_SIZE), :] = ref[0 : RIM * P_SIZE, :]
    for i in range(MIG):

        @pl.when(i < mine_left)
        def _():
            near[rows(E_BAL + RIM - mine_left + i), :] = own[rows(i), :]

        @pl.when(i < mine_right)
        def _():
            near[rows(E_BAL + RIM + i), :] = own[rows(live - mine_right + i), :]

    near[rows(ABOVE), :] = jnp.zeros((P_SIZE, NV), BF16)

    for w in range(E_BAL):
        blk_out[rows(w), :] = matrices[rows(jnp.maximum(shift + w, 0)), :]
    for i in range(MIG):

        @pl.when(i < arrive_left)
        def _():
            x = came[rows(MIG - arrive_left + i, HALF, BLK_IN), :].astype(F32)
            for p in range(2):
                blk_f[pl.ds(p, HALF, stride=2), :] = jnp.where(lane_is(p), x, 0.0)
            blk_out[rows(i), :] = blk_f[...].astype(BF16)

        @pl.when(i < arrive_right)
        def _():
            x = came[rows(i, HALF, ARRIVED + BLK_IN), :].astype(F32)
            for p in range(2):
                blk_f[pl.ds(p, HALF, stride=2), :] = jnp.where(lane_is(p), x, 0.0)
            blk_out[rows(E_BAL - arrive_right + i), :] = blk_f[...].astype(BF16)

    capacity = cap[...]
    weight = wt[...]
    face_rows = faces[...]
    for w in range(E_BAL):
        vector = dirs[rows(jnp.maximum(shift + w, 0)), :].astype(F32)
        if w < MIG:
            arrived = came[rows(jnp.minimum(MIG - arrive_left + w, MIG - 1)), :].astype(F32)
            vector = jnp.where(w < arrive_left, arrived, vector)
        elif w >= E_BAL - MIG:
            arrived = came[rows(jnp.maximum(w - E_BAL + arrive_right, 0), base=ARRIVED), :].astype(F32)
            vector = jnp.where(w >= E_BAL - arrive_right, arrived, vector)
        result = wide_column(capacity, w) * vector + product(near, nbr, blk_out, face_rows, w, ABOVE, ABOVE)
        if LAYER <= w < E_BAL - LAYER:
            rounded = result.astype(BF16)
            first[rows(w - LAYER), :] = rounded
            nxt[rows(w - LAYER), :] = (wide_column(weight, w) * rounded.astype(F32)).astype(BF16)
        else:
            partial[rows(w if w < LAYER else w - E_BAL + 2 * LAYER), :] = result


def product(near, nbr, matrices, face_rows, w, limit, missing):
    mine = near[rows(w), :]
    parts = [mine, mine]
    for k in range(FACES):
        b = nbr[k, 0, w]
        b = jnp.where((b < 0) | (b >= limit), missing, b)
        parts.append(near[rows(b), :])
    lhs = jnp.concatenate([matrices[rows(w), :], face_rows], 1)
    return jnp.dot(lhs, jnp.concatenate(parts, 0), preferred_element_type=F32)


def vertical(nbr, faces, from_above, from_below, i):
    top = i < LAYER
    w = i if top else E_BAL - 2 * LAYER + i
    k = 4 if top else 5
    came = from_above if top else from_below
    inside = nbr[k, 0, w] - (ABOVE if top else BELOW)
    there = (inside >= 0) & (inside < LAYER)
    row = came[rows(jnp.clip(inside, 0, LAYER - 1)), :]
    update = jnp.dot(faces[:, k * P_SIZE : (k + 1) * P_SIZE], row, preferred_element_type=F32)
    return w, jnp.where(there, update, 0.0)


def ends_kernel(
    cnt, nbr, wt, faces, partial, from_above, from_below, nxt, first, to_pair, to_other, to_above, to_below, near, rim,
):
    weight = wt[...]
    for i in range(2 * LAYER):
        w, update = vertical(nbr, faces, from_above, from_below, i)
        rounded = (partial[rows(i), :] + update).astype(BF16)
        first[rows(i), :] = rounded
        onward = (wide_column(weight, w) * rounded.astype(F32)).astype(BF16)
        if i < LAYER:
            rim[rows(i), :] = onward
            to_above[rows(i), :] = onward
        else:
            rim[rows(RIM + i), :] = onward
            to_below[rows(i - LAYER), :] = onward
    span = LAYER * P_SIZE
    rim[span : 3 * span, :] = jnp.concatenate(
        [nxt[0:span, :], nxt[(E_BAL - 3 * LAYER) * P_SIZE : (E_BAL - 2 * LAYER) * P_SIZE, :]], 0
    )
    for out, side in zip((to_pair, to_other), sides(cnt)):
        out[...] = rim[part(side, RIM * P_SIZE), :]
    near[0:span, :] = rim[0:span, :]
    near[span : (E_BAL - LAYER) * P_SIZE, :] = nxt[...]
    near[(E_BAL - LAYER) * P_SIZE :, :] = rim[3 * span :, :]


def second_kernel(cnt, nbr, cap, faces, matrices, mid, ends, own, pair, other, out, partial, near, done, sems):
    near[0 : E_BAL * P_SIZE, :] = own[...]
    for ref, side in zip((pair, other), sides(cnt)):
        at = pl.multiple_of((E_BAL + side * RIM) * P_SIZE, P_SIZE)
        near[pl.ds(at, RIM * P_SIZE), :] = ref[...]
    near[rows(ABOVE), :] = jnp.zeros((P_SIZE, NV), BF16)
    capacity = cap[...]
    face_rows = faces[...]
    copies = []
    for w in range(E_BAL):
        outer = w if w < LAYER else w - E_BAL + 2 * LAYER
        inner = LAYER <= w < E_BAL - LAYER
        vector = mid[rows(w - LAYER), :] if inner else ends[rows(outer), :]
        result = wide_column(capacity, w) * vector.astype(F32) + product(
            near, nbr, matrices, face_rows, w, ABOVE, ABOVE
        )
        if inner:
            done[rows(w - LAYER), :] = result.astype(BF16)
            if (w - LAYER) % PIECE == PIECE - 1:
                span = (w - LAYER + 1 - PIECE) * P_SIZE
                copies.append(
                    pltpu.make_async_copy(
                        done.at[pl.ds(span, PIECE * P_SIZE)],
                        out.at[pl.ds(span + LAYER * P_SIZE, PIECE * P_SIZE)],
                        sems.at[len(copies)],
                    )
                )
                copies[-1].start()
        else:
            partial[rows(outer), :] = result
    for copy in copies:
        copy.wait()


PIECE = 16


def finish_kernel(nbr, faces, partial, from_above, from_below, begun, out, done, sems):
    copies = []
    for i in range(2 * LAYER):
        w, update = vertical(nbr, faces, from_above, from_below, i)
        done[rows(i), :] = (partial[rows(i), :] + update).astype(BF16)
        if i % LAYER == LAYER - 1:
            span = LAYER * P_SIZE
            copies.append(
                pltpu.make_async_copy(
                    done.at[pl.ds((i + 1) * P_SIZE - span, span)],
                    out.at[pl.ds((w + 1) * P_SIZE - span, span)],
                    sems.at[len(copies)],
                )
            )
            copies[-1].start()
    for copy in copies:
        copy.wait()


def smem():
    return pl.BlockSpec(memory_space=pltpu.SMEM)


def vmem():
    return pl.BlockSpec(memory_space=pltpu.VMEM)


def hbm():
    return pl.BlockSpec(memory_space=pltpu.HBM)


def pinned(x):
    return pltpu.with_memory_space_constraint(x, pltpu.HBM)


def held(n, kind=BF16):
    return pltpu.VMEM((n, NV), kind)


def call(kernel, name, ins, arrays, outs, out_specs=None, scratch=(), flops=0, moved=0, aliases=None):
    return pl.pallas_call(
        kernel,
        out_shape=outs,
        in_specs=ins,
        out_specs=out_specs or [vmem()] * len(outs),
        scratch_shapes=list(scratch),
        compiler_params=pltpu.CompilerParams(vmem_limit_bytes=20 * 2**20),
        cost_estimate=pl.CostEstimate(flops=flops, bytes_accessed=moved, transcendentals=0),
        input_output_aliases=aliases or {},
        name=name,
    )(*arrays)


def shifted(value, axis, by):
    peers = lax.axis_size(axis)
    return lax.ppermute(value, axis, [(i, (i + by) % peers) for i in range(peers)])


def swapped(value, first):
    pairs = {i: i for i in range(N_WIDE)}
    for i in range(first, N_WIDE - 1, 2):
        pairs[i], pairs[i + 1] = i + 1, i
    return lax.ppermute(value, "wide", list(pairs.items()))


def per_device(soil_state, directions, blocks, send_left, send_right, neighbours, face_blocks):
    soil = soil_state[0]
    dirs = directions.reshape(E_DEV * P_SIZE, NV)
    rows_of = blocks[0]
    column = held(P_SIZE, F32)
    layer, rim = held(LAYER * P_SIZE), held(RIM * P_SIZE)
    slots = held(E_DEV * P_SIZE)
    inner = held((E_BAL - 2 * LAYER) * P_SIZE)

    to_pair, to_other, cap_own, wt_own, cnt, nbr = call(
        prepare_kernel, "prepare", [hbm()] * 6,
        [pinned(x) for x in (send_left, send_right, jnp.swapaxes(neighbours, 0, 1), soil, dirs, rows_of)],
        (held(MESSAGE), held(MESSAGE), column, column, pltpu.SMEM((PARITY + 1,), jnp.int32), pltpu.SMEM((FACES, 1, E_BAL), jnp.int32)),
        [vmem()] * 4 + [smem()] * 2,
        (
            pltpu.SMEM((N_WIDE,), jnp.int32), pltpu.SMEM((N_WIDE,), jnp.int32),
            pltpu.VMEM((E_DEV, 2 * NV), BF16), pltpu.VMEM((2 * NV, NV), F32),
            pltpu.VMEM((HEAD * P_SIZE, NV), BF16), pltpu.VMEM((TAIL * P_SIZE, NV), BF16),
            pltpu.VMEM((16, P_SIZE * P_SIZE), BF16), pltpu.VMEM((BLK_TAIL, P_SIZE * P_SIZE), BF16),
            pltpu.VMEM((48 * HALF, NV), F32), held(2 * MESSAGE), pltpu.SemaphoreType.DMA((8,)),
        ),
    )
    pair = swapped(to_pair, 0)
    other = swapped(to_other, 1)

    own, matrices, faces = call(
        own_kernel, "own", [vmem()] * 4, (wt_own, dirs, rows_of, face_blocks),
        (slots, slots, pltpu.VMEM((P_SIZE, FACES * P_SIZE), BF16)),
        scratch=(pltpu.VMEM((16 * P_SIZE, NV), F32),),
        flops=10**9, moved=6 * 2**20,
    )

    above, below, came, cap, wt = call(
        arrive_kernel, "arrive", [smem()] + [vmem()] * 5, (cnt, cap_own, wt_own, pair, other, own),
        (layer, layer, held(2 * ARRIVED), column, column),
        scratch=(held(2 * MIG * P_SIZE), pltpu.VMEM((2 * NV, NV), F32)),
    )
    from_below = shifted(above, "narrow", -1)
    from_above = shifted(below, "narrow", 1)

    blk, partial, first, nxt = call(
        first_kernel, "first", [smem()] * 2 + [vmem()] * 11,
        (cnt, nbr, cap, wt, faces, dirs, own, matrices, came, above, below, pair, other),
        (held(E_BAL * P_SIZE), held(2 * LAYER * P_SIZE, F32), inner, inner),
        scratch=(held((ABOVE + 1) * P_SIZE), held(P_SIZE, F32)),
        flops=2 * 10**9, moved=8 * 2**20,
    )
    ends, go_pair, go_other, go_above, go_below, onward = call(
        ends_kernel, "ends", [smem()] * 2 + [vmem()] * 6, (cnt, nbr, wt, faces, partial, from_above, from_below, nxt),
        (held(2 * LAYER * P_SIZE), rim, rim, layer, layer, held(E_BAL * P_SIZE)),
        scratch=(held(2 * RIM * P_SIZE),),
    )
    pair = swapped(go_pair, 0)
    other = swapped(go_other, 1)
    came_below = shifted(go_above, "narrow", -1)
    came_above = shifted(go_below, "narrow", 1)
    result = jax.ShapeDtypeStruct((E_BAL * P_SIZE, NV), BF16)
    begun, partial = call(
        second_kernel, "second", [smem()] * 2 + [vmem()] * 8,
        (cnt, nbr, cap, faces, blk, first, ends, onward, pair, other),
        (result, held(2 * LAYER * P_SIZE, F32)), [hbm(), vmem()],
        scratch=(
            held((ABOVE + 1) * P_SIZE), held((E_BAL - 2 * LAYER) * P_SIZE),
            pltpu.SemaphoreType.DMA(((E_BAL - 2 * LAYER) // PIECE,)),
        ),
        flops=10**9, moved=6 * 2**20,
    )
    (out,) = call(
        finish_kernel, "finish", [smem()] + [vmem()] * 4 + [hbm()],
        (nbr, faces, partial, came_above, came_below, begun),
        (result,), [hbm()],
        scratch=(held(2 * LAYER * P_SIZE), pltpu.SemaphoreType.DMA((2,))),
        aliases={5: 0},
    )
    return out.reshape(1, E_BAL, P_SIZE, NV)


def solution(mesh):
    in_specs = (
        P("narrow", "wide", None),
        P("narrow", "wide", None, None),
        P("narrow", "wide", None),
        P(),
        P(),
        P("narrow", None, "wide"),
        P(),
    )
    out_specs = P("narrow", "wide", None, None)
    return jax.shard_map(
        per_device, mesh=mesh, in_specs=in_specs, out_specs=out_specs, check_vma=False
    )
```

```python
import jax
import jax.numpy as jnp
from jax import lax
from jax.experimental import pallas as pl
from jax.experimental.pallas import tpu as pltpu
from jax.sharding import PartitionSpec as P

P_SIZE = 64
FACES = 6
NV = 128
E_BAL = 64
MIG = 8
RIM = 16
LAYER = 8
E_DEV = 80
N_WIDE = 64
COLS = 4
HALF = P_SIZE // 2
ABOVE = E_BAL + 2 * RIM
BELOW = ABOVE + LAYER
MISSING = BELOW + LAYER

DIR_AT = RIM * P_SIZE
BLK_AT = DIR_AT + MIG * P_SIZE
SOIL_AT = BLK_AT + MIG * HALF
MESSAGE = SOIL_AT + 2 * MIG

moisture_range = 0.4
time_step = 0.5

F32 = jnp.float32
BF16 = jnp.bfloat16


def closures(pressure, inverse_entry, pore_index, conduct_sat):
    exponent = 1.0 - 1.0 / pore_index
    log_scaled = jnp.log(-inverse_entry * pressure)
    power = jnp.exp(pore_index * log_scaled)
    log_denom = jnp.log1p(power)
    saturation = jnp.exp(-exponent * log_denom)
    ratio_log = pore_index * log_scaled - log_denom
    relative = jnp.sqrt(saturation) * jnp.square(1.0 - jnp.exp(exponent * ratio_log))
    capacity = (
        moisture_range
        * inverse_entry
        * pore_index
        * exponent
        * jnp.exp((pore_index - 1.0) * log_scaled - (exponent + 1.0) * log_denom)
        / time_step
    )
    return capacity, conduct_sat * relative


def closures_by_column(soil_rows):
    cols = [jnp.transpose(soil_rows[k * NV : (k + 1) * NV]) for k in range(2)]
    fields = [cols[i // 2][i % 2 * P_SIZE : (i % 2 + 1) * P_SIZE] for i in range(4)]
    return closures(*fields)


def counts(send_left, send_right):
    t = lax.axis_index("wide")
    before = lax.rem(t + N_WIDE - 1, N_WIDE)
    after = lax.rem(t + 1, N_WIDE)
    mine_left = send_left[t]
    mine_right = send_right[t]
    arrive_left = jnp.where(t > 0, send_right[before], 0)
    arrive_right = jnp.where(t < N_WIDE - 1, send_left[after], 0)
    return mine_left, mine_right, arrive_left, arrive_right


PARITY = 4


def sides(cnt):
    return 1 - cnt[PARITY], cnt[PARITY]


def part(side, size):
    return pl.ds(pl.multiple_of(side * size, size if size % 16 == 0 else 16), size)


def moves(cnt):
    mine_left, mine_right, arrive_left, arrive_right = (cnt[i] for i in range(4))
    live = E_BAL + mine_left + mine_right - arrive_left - arrive_right
    return mine_left, mine_right, arrive_left, arrive_right, live


def rows(index, size=P_SIZE, base=0):
    if isinstance(index, int):
        return pl.ds(base + index * size, size)
    return pl.ds(pl.multiple_of(base + index * size, 16), size)


def wide_column(columns, lane):
    return jnp.broadcast_to(columns[:, lane : lane + 1], (P_SIZE, NV))


def lane_is(p):
    return (lax.broadcasted_iota(jnp.int32, (1, NV), 1) >= P_SIZE) == bool(p)


HEAD = MIG + RIM
TAIL = E_DEV - 40
BLK_TAIL = E_DEV - 32


def prepare_kernel(
    sl, sr, nbr, soil, dirs, blocks, to_other, to_pair, cap_out, wt_out, cnt, nbr_out,
    sl_s, sr_s, soil_b, soil_f, dir_head, dir_tail, blk_head, blk_tail, blk_f, message, sems,
):
    to_left = message.at[pl.ds(0, MESSAGE)]
    to_right = message.at[pl.ds(MESSAGE, MESSAGE)]
    copies = [
        pltpu.make_async_copy(source, target, sems.at[i])
        for i, (source, target) in enumerate((
            (soil, soil_b),
            (sl, sl_s),
            (sr, sr_s),
            (dirs.at[pl.ds(0, HEAD * P_SIZE)], dir_head),
            (dirs.at[pl.ds((E_DEV - TAIL) * P_SIZE, TAIL * P_SIZE)], dir_tail),
            (blocks.at[pl.ds(0, 16)], blk_head),
            (blocks.at[pl.ds(E_DEV - BLK_TAIL, BLK_TAIL)], blk_tail),
            (nbr, nbr_out),
        ))
    ]
    for copy in copies:
        copy.start()
    for k in range(2):
        soil_f[k * NV + E_DEV : (k + 1) * NV, :] = jnp.full((NV - E_DEV, NV), 1.0, F32)
    copies[0].wait()
    for k in range(2):
        soil_f[k * NV : k * NV + E_DEV, :] = soil_b[:, k * NV : (k + 1) * NV].astype(F32)
    capacity, weight = closures_by_column(soil_f[...])
    wt_out[...] = weight
    cap_out[...] = capacity
    copies[1].wait()
    copies[2].wait()
    for i, n in enumerate(counts(sl_s, sr_s)):
        cnt[i] = n
    cnt[PARITY] = lax.rem(lax.axis_index("wide"), 2)
    mine_left, mine_right, arrive_left, arrive_right, live = moves(cnt)
    middle = mine_left - arrive_left
    tail = live - MIG
    here = pltpu.roll(weight, lax.rem(NV - middle, NV), 1)
    copies[3].wait()
    copies[4].wait()
    for i in range(RIM):
        s = middle + E_BAL - RIM + i - (E_DEV - TAIL)
        to_right[rows(i), :] = (wide_column(here, E_BAL - RIM + i) * dir_tail[rows(s), :].astype(F32)).astype(BF16)
        s = jnp.maximum(middle + i, 0)
        to_left[rows(i), :] = (wide_column(here, i) * dir_head[rows(s), :].astype(F32)).astype(BF16)
    at = pl.multiple_of((tail - (E_DEV - TAIL)) * P_SIZE, P_SIZE)
    to_right[pl.ds(DIR_AT, MIG * P_SIZE), :] = dir_tail[pl.ds(at, MIG * P_SIZE), :]
    to_left[pl.ds(DIR_AT, MIG * P_SIZE), :] = dir_head[0 : MIG * P_SIZE, :]
    for out, first in ((to_right, tail), (to_left, 0)):
        both = jnp.concatenate([soil_f[pl.ds(k * NV + first, MIG), :] for k in range(2)], 0)
        out[pl.ds(SOIL_AT, 2 * MIG), :] = both.astype(BF16)
    copies[5].wait()
    copies[6].wait()
    start = E_DEV - BLK_TAIL
    group = jnp.minimum(lax.div(tail - start, 16) * 16, BLK_TAIL - 32)
    for g in range(3):
        for c in range(HALF):
            lanes = slice(c * NV, (c + 1) * NV)
            if g == 0:
                x = blk_head[:, lanes]
            else:
                x = blk_tail[pl.ds(pl.multiple_of(group + 16 * (g - 1), 16), 16), lanes]
            blk_f[pl.ds(g * 16 * HALF + c, 16, stride=HALF), :] = x.astype(F32)
    at = pl.multiple_of((16 + tail - start - group) * HALF, HALF)
    to_right[pl.ds(BLK_AT, MIG * HALF), :] = blk_f[pl.ds(at, MIG * HALF), :].astype(BF16)
    to_left[pl.ds(BLK_AT, MIG * HALF), :] = blk_f[0 : MIG * HALF, :].astype(BF16)
    for out, side in zip((to_pair, to_other), sides(cnt)):
        out[...] = message[part(side, MESSAGE), :]
    copies[7].wait()


def own_kernel(wt, dirs, blocks, face_blocks, weighted, matrices, faces, blk_f):
    for k in range(FACES):
        faces[:, k * P_SIZE : (k + 1) * P_SIZE] = -face_blocks[k]
    weight = wt[...]
    for s in range(E_DEV):
        weighted[rows(s), :] = (wide_column(weight, s) * dirs[rows(s), :].astype(F32)).astype(BF16)
    for g in range(E_DEV // 16):
        for c in range(HALF):
            x = blocks[g * 16 : (g + 1) * 16, c * NV : (c + 1) * NV].astype(F32)
            for p in range(2):
                blk_f[pl.ds(2 * c + p, 16, stride=P_SIZE), :] = jnp.where(lane_is(p), x, 0.0)
        matrices[g * 16 * P_SIZE : (g + 1) * 16 * P_SIZE, :] = blk_f[...].astype(BF16)


ARRIVED = MESSAGE - DIR_AT
BLK_IN = BLK_AT - DIR_AT
SOIL_IN = SOIL_AT - DIR_AT


def arrive_kernel(other, pair, cnt, cap_own, wt_own, own, to_above, to_below, came, cap_out, wt_out, moved, soil_f):
    mine_left, mine_right, arrive_left, arrive_right, live = moves(cnt)
    for ref, side in zip((pair, other), sides(cnt)):
        came[part(side, ARRIVED), :] = ref[DIR_AT:, :]
    soil_f[...] = jnp.full((2 * NV, NV), 1.0, F32)
    for side in range(2):
        x = came[pl.ds(side * ARRIVED + SOIL_IN, 2 * MIG), :].astype(F32)
        for k in range(2):
            soil_f[k * NV + side * MIG : k * NV + (side + 1) * MIG, :] = x[k * MIG : (k + 1) * MIG]
    capacity, weight = closures_by_column(soil_f[...])
    lane = lax.broadcasted_iota(jnp.int32, (P_SIZE, NV), 1)
    for out, mine, theirs in ((cap_out, cap_own, capacity), (wt_out, wt_own, weight)):
        middle = pltpu.roll(mine[...], lax.rem(arrive_left - mine_left + NV, NV), 1)
        left = pltpu.roll(theirs, lax.rem(arrive_left - MIG + NV, NV), 1)
        right = pltpu.roll(theirs, E_BAL - arrive_right - MIG, 1)
        out[...] = jnp.where(lane < arrive_left, left, jnp.where(lane < E_BAL - arrive_right, middle, right))
    for i in range(2 * MIG):
        raw = came[rows(i % MIG, base=i // MIG * ARRIVED), :]
        moved[rows(i), :] = (wide_column(weight, i) * raw.astype(F32)).astype(BF16)
    shift = mine_left - arrive_left
    for i in range(LAYER):
        here = own[rows(jnp.maximum(shift + i, 0)), :].astype(F32)
        came = moved[rows(jnp.minimum(MIG - arrive_left + i, MIG - 1)), :].astype(F32)
        to_above[rows(i), :] = jnp.where(i < arrive_left, came, here).astype(BF16)
        w = E_BAL - LAYER + i
        here = own[rows(shift + w), :].astype(F32)
        came = moved[rows(jnp.maximum(w - E_BAL + arrive_right, 0) + MIG), :].astype(F32)
        to_below[rows(i), :] = jnp.where(w >= E_BAL - arrive_right, came, here).astype(BF16)


def first_kernel(
    cnt, nbr, cap, wt, faces, dirs, own, matrices, came, above, below, pair, other,
    blk_out, partial, first, nxt, near, blk_f,
):
    mine_left, mine_right, arrive_left, arrive_right, live = moves(cnt)
    shift = mine_left - arrive_left
    for w in range(E_BAL):
        if w < LAYER:
            near[rows(w), :] = above[rows(w), :]
        elif w >= E_BAL - LAYER:
            near[rows(w), :] = below[rows(w - E_BAL + LAYER), :]
        else:
            near[rows(w), :] = own[rows(shift + w), :]
    for ref, side in zip((pair, other), sides(cnt)):
        at = pl.multiple_of((E_BAL + side * RIM) * P_SIZE, P_SIZE)
        near[pl.ds(at, RIM * P_SIZE), :] = ref[0 : RIM * P_SIZE, :]
    for i in range(MIG):

        @pl.when(i < mine_left)
        def _():
            near[rows(E_BAL + RIM - mine_left + i), :] = own[rows(i), :]

        @pl.when(i < mine_right)
        def _():
            near[rows(E_BAL + RIM + i), :] = own[rows(live - mine_right + i), :]

    near[rows(ABOVE), :] = jnp.zeros((P_SIZE, NV), BF16)

    for w in range(E_BAL):
        blk_out[rows(w), :] = matrices[rows(jnp.maximum(shift + w, 0)), :]
    for i in range(MIG):

        @pl.when(i < arrive_left)
        def _():
            x = came[rows(MIG - arrive_left + i, HALF, BLK_IN), :].astype(F32)
            for p in range(2):
                blk_f[pl.ds(p, HALF, stride=2), :] = jnp.where(lane_is(p), x, 0.0)
            blk_out[rows(i), :] = blk_f[...].astype(BF16)

        @pl.when(i < arrive_right)
        def _():
            x = came[rows(i, HALF, ARRIVED + BLK_IN), :].astype(F32)
            for p in range(2):
                blk_f[pl.ds(p, HALF, stride=2), :] = jnp.where(lane_is(p), x, 0.0)
            blk_out[rows(E_BAL - arrive_right + i), :] = blk_f[...].astype(BF16)

    capacity = cap[...]
    weight = wt[...]
    face_rows = faces[...]
    for w in range(E_BAL):
        vector = dirs[rows(jnp.maximum(shift + w, 0)), :].astype(F32)
        if w < MIG:
            arrived = came[rows(jnp.minimum(MIG - arrive_left + w, MIG - 1)), :].astype(F32)
            vector = jnp.where(w < arrive_left, arrived, vector)
        elif w >= E_BAL - MIG:
            arrived = came[rows(jnp.maximum(w - E_BAL + arrive_right, 0), base=ARRIVED), :].astype(F32)
            vector = jnp.where(w >= E_BAL - arrive_right, arrived, vector)
        result = wide_column(capacity, w) * vector + product(near, nbr, blk_out, face_rows, w, ABOVE, ABOVE)
        if LAYER <= w < E_BAL - LAYER:
            rounded = result.astype(BF16)
            first[rows(w - LAYER), :] = rounded
            nxt[rows(w - LAYER), :] = (wide_column(weight, w) * rounded.astype(F32)).astype(BF16)
        else:
            partial[rows(w if w < LAYER else w - E_BAL + 2 * LAYER), :] = result


def product(near, nbr, matrices, face_rows, w, limit, missing):
    mine = near[rows(w), :]
    parts = [mine, mine]
    for k in range(FACES):
        b = nbr[k, 0, w]
        b = jnp.where((b < 0) | (b >= limit), missing, b)
        parts.append(near[rows(b), :])
    lhs = jnp.concatenate([matrices[rows(w), :], face_rows], 1)
    return jnp.dot(lhs, jnp.concatenate(parts, 0), preferred_element_type=F32)


def vertical(nbr, faces, from_above, from_below, i):
    top = i < LAYER
    w = i if top else E_BAL - 2 * LAYER + i
    k = 4 if top else 5
    came = from_above if top else from_below
    inside = nbr[k, 0, w] - (ABOVE if top else BELOW)
    there = (inside >= 0) & (inside < LAYER)
    row = came[rows(jnp.clip(inside, 0, LAYER - 1)), :]
    update = jnp.dot(faces[:, k * P_SIZE : (k + 1) * P_SIZE], row, preferred_element_type=F32)
    return w, jnp.where(there, update, 0.0)


def ends_kernel(
    cnt, nbr, wt, faces, partial, from_above, from_below, nxt, first, to_other, to_pair, to_above, to_below, near, rim,
):
    weight = wt[...]
    for i in range(2 * LAYER):
        w, update = vertical(nbr, faces, from_above, from_below, i)
        rounded = (partial[rows(i), :] + update).astype(BF16)
        first[rows(i), :] = rounded
        onward = (wide_column(weight, w) * rounded.astype(F32)).astype(BF16)
        if i < LAYER:
            rim[rows(i), :] = onward
            to_above[rows(i), :] = onward
        else:
            rim[rows(RIM + i), :] = onward
            to_below[rows(i - LAYER), :] = onward
    span = LAYER * P_SIZE
    rim[span : 3 * span, :] = jnp.concatenate(
        [nxt[0:span, :], nxt[(E_BAL - 3 * LAYER) * P_SIZE : (E_BAL - 2 * LAYER) * P_SIZE, :]], 0
    )
    for out, side in zip((to_pair, to_other), sides(cnt)):
        out[...] = rim[part(side, RIM * P_SIZE), :]
    near[0:span, :] = rim[0:span, :]
    near[span : (E_BAL - LAYER) * P_SIZE, :] = nxt[...]
    near[(E_BAL - LAYER) * P_SIZE :, :] = rim[3 * span :, :]


def second_kernel(other, pair, cnt, nbr, cap, faces, matrices, mid, ends, own, out, partial, near, done, sems):
    near[0 : E_BAL * P_SIZE, :] = own[...]
    for ref, side in zip((pair, other), sides(cnt)):
        at = pl.multiple_of((E_BAL + side * RIM) * P_SIZE, P_SIZE)
        near[pl.ds(at, RIM * P_SIZE), :] = ref[...]
    near[rows(ABOVE), :] = jnp.zeros((P_SIZE, NV), BF16)
    capacity = cap[...]
    face_rows = faces[...]
    copies = []
    for w in range(E_BAL):
        outer = w if w < LAYER else w - E_BAL + 2 * LAYER
        inner = LAYER <= w < E_BAL - LAYER
        vector = mid[rows(w - LAYER), :] if inner else ends[rows(outer), :]
        result = wide_column(capacity, w) * vector.astype(F32) + product(
            near, nbr, matrices, face_rows, w, ABOVE, ABOVE
        )
        if inner:
            done[rows(w - LAYER), :] = result.astype(BF16)
            if (w - LAYER) % PIECE == PIECE - 1:
                span = (w - LAYER + 1 - PIECE) * P_SIZE
                copies.append(
                    pltpu.make_async_copy(
                        done.at[pl.ds(span, PIECE * P_SIZE)],
                        out.at[pl.ds(span + LAYER * P_SIZE, PIECE * P_SIZE)],
                        sems.at[len(copies)],
                    )
                )
                copies[-1].start()
        else:
            partial[rows(outer), :] = result
    for copy in copies:
        copy.wait()


PIECE = 16


def finish_kernel(nbr, faces, partial, from_above, from_below, begun, out, done, sems):
    copies = []
    for i in range(2 * LAYER):
        w, update = vertical(nbr, faces, from_above, from_below, i)
        done[rows(i), :] = (partial[rows(i), :] + update).astype(BF16)
        if i % LAYER == LAYER - 1:
            span = LAYER * P_SIZE
            copies.append(
                pltpu.make_async_copy(
                    done.at[pl.ds((i + 1) * P_SIZE - span, span)],
                    out.at[pl.ds((w + 1) * P_SIZE - span, span)],
                    sems.at[len(copies)],
                )
            )
            copies[-1].start()
    for copy in copies:
        copy.wait()


def smem():
    return pl.BlockSpec(memory_space=pltpu.SMEM)


def vmem():
    return pl.BlockSpec(memory_space=pltpu.VMEM)


def hbm():
    return pl.BlockSpec(memory_space=pltpu.HBM)


def pinned(x):
    return pltpu.with_memory_space_constraint(x, pltpu.HBM)


def held(n, kind=BF16):
    return pltpu.VMEM((n, NV), kind)


def call(kernel, name, ins, arrays, outs, out_specs=None, scratch=(), flops=0, moved=0, aliases=None):
    return pl.pallas_call(
        kernel,
        out_shape=outs,
        in_specs=ins,
        out_specs=out_specs or [vmem()] * len(outs),
        scratch_shapes=list(scratch),
        compiler_params=pltpu.CompilerParams(vmem_limit_bytes=20 * 2**20),
        cost_estimate=pl.CostEstimate(flops=flops, bytes_accessed=moved, transcendentals=0),
        input_output_aliases=aliases or {},
        name=name,
    )(*arrays)


def shifted(value, axis, by):
    peers = lax.axis_size(axis)
    return lax.ppermute(value, axis, [(i, (i + by) % peers) for i in range(peers)])


def swapped(value, first):
    pairs = []
    for t in range(N_WIDE):
        partner = t + 1 if (t - first) % 2 == 0 else t - 1
        for c in range(COLS):
            target = (partner, c) if 0 <= partner < N_WIDE else (t, c ^ 1)
            pairs.append((t * COLS + c, target[0] * COLS + target[1]))
    return lax.ppermute(value, ("wide", "narrow"), pairs)


def per_device(soil_state, directions, blocks, send_left, send_right, neighbours, face_blocks):
    soil = soil_state[0]
    dirs = directions.reshape(E_DEV * P_SIZE, NV)
    rows_of = blocks[0]
    column = held(P_SIZE, F32)
    layer, rim = held(LAYER * P_SIZE), held(RIM * P_SIZE)
    slots = held(E_DEV * P_SIZE)
    inner = held((E_BAL - 2 * LAYER) * P_SIZE)

    to_other, to_pair, cap_own, wt_own, cnt, nbr = call(
        prepare_kernel, "prepare", [hbm()] * 6,
        [pinned(x) for x in (send_left, send_right, jnp.swapaxes(neighbours, 0, 1), soil, dirs, rows_of)],
        (held(MESSAGE), held(MESSAGE), column, column, pltpu.SMEM((PARITY + 1,), jnp.int32), pltpu.SMEM((FACES, 1, E_BAL), jnp.int32)),
        [vmem()] * 4 + [smem()] * 2,
        (
            pltpu.SMEM((N_WIDE,), jnp.int32), pltpu.SMEM((N_WIDE,), jnp.int32),
            pltpu.VMEM((E_DEV, 2 * NV), BF16), pltpu.VMEM((2 * NV, NV), F32),
            pltpu.VMEM((HEAD * P_SIZE, NV), BF16), pltpu.VMEM((TAIL * P_SIZE, NV), BF16),
            pltpu.VMEM((16, P_SIZE * P_SIZE), BF16), pltpu.VMEM((BLK_TAIL, P_SIZE * P_SIZE), BF16),
            pltpu.VMEM((48 * HALF, NV), F32), held(2 * MESSAGE), pltpu.SemaphoreType.DMA((8,)),
        ),
    )
    other = swapped(to_other, 1)
    pair = swapped(to_pair, 0)

    own, matrices, faces = call(
        own_kernel, "own", [vmem()] * 4, (wt_own, dirs, rows_of, face_blocks),
        (slots, slots, pltpu.VMEM((P_SIZE, FACES * P_SIZE), BF16)),
        scratch=(pltpu.VMEM((16 * P_SIZE, NV), F32),),
        flops=10**9, moved=6 * 2**20,
    )

    above, below, came, cap, wt = call(
        arrive_kernel, "arrive", [vmem()] * 2 + [smem()] + [vmem()] * 3, (other, pair, cnt, cap_own, wt_own, own),
        (layer, layer, held(2 * ARRIVED), column, column),
        scratch=(held(2 * MIG * P_SIZE), pltpu.VMEM((2 * NV, NV), F32)),
    )
    from_below = shifted(above, "narrow", -1)
    from_above = shifted(below, "narrow", 1)

    blk, partial, first, nxt = call(
        first_kernel, "first", [smem()] * 2 + [vmem()] * 11,
        (cnt, nbr, cap, wt, faces, dirs, own, matrices, came, above, below, pair, other),
        (held(E_BAL * P_SIZE), held(2 * LAYER * P_SIZE, F32), inner, inner),
        scratch=(held((ABOVE + 1) * P_SIZE), held(P_SIZE, F32)),
        flops=2 * 10**9, moved=8 * 2**20,
    )
    ends, go_other, go_pair, go_above, go_below, onward = call(
        ends_kernel, "ends", [smem()] * 2 + [vmem()] * 6, (cnt, nbr, wt, faces, partial, from_above, from_below, nxt),
        (held(2 * LAYER * P_SIZE), rim, rim, layer, layer, held(E_BAL * P_SIZE)),
        scratch=(held(2 * RIM * P_SIZE),),
    )
    other = swapped(go_other, 1)
    pair = swapped(go_pair, 0)
    came_below = shifted(go_above, "narrow", -1)
    came_above = shifted(go_below, "narrow", 1)
    result = jax.ShapeDtypeStruct((E_BAL * P_SIZE, NV), BF16)
    begun, partial = call(
        second_kernel, "second", [vmem()] * 2 + [smem()] * 2 + [vmem()] * 6,
        (other, pair, cnt, nbr, cap, faces, blk, first, ends, onward),
        (result, held(2 * LAYER * P_SIZE, F32)), [hbm(), vmem()],
        scratch=(
            held((ABOVE + 1) * P_SIZE), held((E_BAL - 2 * LAYER) * P_SIZE),
            pltpu.SemaphoreType.DMA(((E_BAL - 2 * LAYER) // PIECE,)),
        ),
        flops=10**9, moved=6 * 2**20,
    )
    (out,) = call(
        finish_kernel, "finish", [smem()] + [vmem()] * 4 + [hbm()],
        (nbr, faces, partial, came_above, came_below, begun),
        (result,), [hbm()],
        scratch=(held(2 * LAYER * P_SIZE), pltpu.SemaphoreType.DMA((2,))),
        aliases={5: 0},
    )
    return out.reshape(1, E_BAL, P_SIZE, NV)


def solution(mesh):
    in_specs = (
        P("narrow", "wide", None),
        P("narrow", "wide", None, None),
        P("narrow", "wide", None),
        P(),
        P(),
        P("narrow", None, "wide"),
        P(),
    )
    out_specs = P("narrow", "wide", None, None)
    return jax.shard_map(
        per_device, mesh=mesh, in_specs=in_specs, out_specs=out_specs, check_vma=False
    )
```

```python
import jax
import jax.numpy as jnp
from jax import lax
from jax.experimental import pallas as pl
from jax.experimental.pallas import tpu as pltpu
from jax.sharding import PartitionSpec as P

P_SIZE = 64
FACES = 6
NV = 128
E_BAL = 64
MIG = 8
RIM = 16
LAYER = 8
E_DEV = 80
N_WIDE = 64
COLS = 4
HALF = P_SIZE // 2
ABOVE = E_BAL + 2 * RIM
BELOW = ABOVE + LAYER
MISSING = BELOW + LAYER

DIR_AT = RIM * P_SIZE
BLK_AT = DIR_AT + MIG * P_SIZE
SOIL_AT = BLK_AT + MIG * HALF
MESSAGE = SOIL_AT + 2 * MIG

moisture_range = 0.4
time_step = 0.5

F32 = jnp.float32
BF16 = jnp.bfloat16


def closures(pressure, inverse_entry, pore_index, conduct_sat):
    exponent = 1.0 - 1.0 / pore_index
    log_scaled = jnp.log(-inverse_entry * pressure)
    power = jnp.exp(pore_index * log_scaled)
    log_denom = jnp.log1p(power)
    saturation = jnp.exp(-exponent * log_denom)
    ratio_log = pore_index * log_scaled - log_denom
    relative = jnp.sqrt(saturation) * jnp.square(1.0 - jnp.exp(exponent * ratio_log))
    capacity = (
        moisture_range
        * inverse_entry
        * pore_index
        * exponent
        * jnp.exp((pore_index - 1.0) * log_scaled - (exponent + 1.0) * log_denom)
        / time_step
    )
    return capacity, conduct_sat * relative


def closures_by_column(soil_rows):
    cols = [jnp.transpose(soil_rows[k * NV : (k + 1) * NV]) for k in range(2)]
    fields = [cols[i // 2][i % 2 * P_SIZE : (i % 2 + 1) * P_SIZE] for i in range(4)]
    return closures(*fields)


def counts(send_left, send_right):
    t = lax.axis_index("wide")
    before = lax.rem(t + N_WIDE - 1, N_WIDE)
    after = lax.rem(t + 1, N_WIDE)
    mine_left = send_left[t]
    mine_right = send_right[t]
    arrive_left = jnp.where(t > 0, send_right[before], 0)
    arrive_right = jnp.where(t < N_WIDE - 1, send_left[after], 0)
    return mine_left, mine_right, arrive_left, arrive_right


PARITY = 4


def sides(cnt):
    return 1 - cnt[PARITY], cnt[PARITY]


def part(side, size):
    return pl.ds(pl.multiple_of(side * size, size if size % 16 == 0 else 16), size)


def moves(cnt):
    mine_left, mine_right, arrive_left, arrive_right = (cnt[i] for i in range(4))
    live = E_BAL + mine_left + mine_right - arrive_left - arrive_right
    return mine_left, mine_right, arrive_left, arrive_right, live


def rows(index, size=P_SIZE, base=0):
    if isinstance(index, int):
        return pl.ds(base + index * size, size)
    return pl.ds(pl.multiple_of(base + index * size, 16), size)


def wide_column(columns, lane):
    return jnp.broadcast_to(columns[:, lane : lane + 1], (P_SIZE, NV))


def lane_is(p):
    return (lax.broadcasted_iota(jnp.int32, (1, NV), 1) >= P_SIZE) == bool(p)


PITCH = HALF + 1
HEAD = MIG + RIM
TAIL = E_DEV - 40
BLK_TAIL = E_DEV - 32


def prepare_kernel(
    sl, sr, nbr, soil, dirs, blocks, to_other, to_pair, cap_out, wt_out, cnt, nbr_out,
    sl_s, sr_s, soil_b, soil_f, dir_head, dir_tail, blk_head, blk_tail, blk_f, message, sems,
):
    to_left = message.at[pl.ds(0, MESSAGE)]
    to_right = message.at[pl.ds(MESSAGE, MESSAGE)]
    copies = [
        pltpu.make_async_copy(source, target, sems.at[i])
        for i, (source, target) in enumerate((
            (soil, soil_b),
            (sl, sl_s),
            (sr, sr_s),
            (dirs.at[pl.ds(0, HEAD * P_SIZE)], dir_head),
            (dirs.at[pl.ds((E_DEV - TAIL) * P_SIZE, TAIL * P_SIZE)], dir_tail),
            (blocks.at[pl.ds(0, 16)], blk_head),
            (blocks.at[pl.ds(E_DEV - BLK_TAIL, BLK_TAIL)], blk_tail),
            (nbr, nbr_out),
        ))
    ]
    for copy in copies:
        copy.start()
    for k in range(2):
        soil_f[k * NV + E_DEV : (k + 1) * NV, :] = jnp.full((NV - E_DEV, NV), 1.0, F32)
    copies[0].wait()
    for k in range(2):
        soil_f[k * NV : k * NV + E_DEV, :] = soil_b[:, k * NV : (k + 1) * NV].astype(F32)
    capacity, weight = closures_by_column(soil_f[...])
    wt_out[...] = weight
    cap_out[...] = capacity
    copies[1].wait()
    copies[2].wait()
    for i, n in enumerate(counts(sl_s, sr_s)):
        cnt[i] = n
    cnt[PARITY] = lax.rem(lax.axis_index("wide"), 2)
    mine_left, mine_right, arrive_left, arrive_right, live = moves(cnt)
    middle = mine_left - arrive_left
    tail = live - MIG
    here = pltpu.roll(weight, lax.rem(NV - middle, NV), 1)
    copies[3].wait()
    copies[4].wait()
    for i in range(RIM):
        s = middle + E_BAL - RIM + i - (E_DEV - TAIL)
        to_right[rows(i), :] = (wide_column(here, E_BAL - RIM + i) * dir_tail[rows(s), :].astype(F32)).astype(BF16)
        s = jnp.maximum(middle + i, 0)
        to_left[rows(i), :] = (wide_column(here, i) * dir_head[rows(s), :].astype(F32)).astype(BF16)
    at = pl.multiple_of((tail - (E_DEV - TAIL)) * P_SIZE, P_SIZE)
    to_right[pl.ds(DIR_AT, MIG * P_SIZE), :] = dir_tail[pl.ds(at, MIG * P_SIZE), :]
    to_left[pl.ds(DIR_AT, MIG * P_SIZE), :] = dir_head[0 : MIG * P_SIZE, :]
    for out, first in ((to_right, tail), (to_left, 0)):
        both = jnp.concatenate([soil_f[pl.ds(k * NV + first, MIG), :] for k in range(2)], 0)
        out[pl.ds(SOIL_AT, 2 * MIG), :] = both.astype(BF16)
    copies[5].wait()
    copies[6].wait()
    start = E_DEV - BLK_TAIL
    group = jnp.minimum(lax.div(tail - start, 16) * 16, BLK_TAIL - 32)
    for g in range(3):
        for c in range(HALF):
            lanes = slice(c * NV, (c + 1) * NV)
            if g == 0:
                x = blk_head[:, lanes]
            else:
                x = blk_tail[pl.ds(pl.multiple_of(group + 16 * (g - 1), 16), 16), lanes]
            blk_f[pl.ds(g * 16 * PITCH + c, 16, stride=PITCH), :] = x.astype(F32)
    for i in range(MIG):
        at = (16 + tail - start - group + i) * PITCH
        to_right[rows(i, HALF, BLK_AT), :] = blk_f[pl.ds(at, HALF), :].astype(BF16)
        to_left[rows(i, HALF, BLK_AT), :] = blk_f[pl.ds(i * PITCH, HALF), :].astype(BF16)
    for out, side in zip((to_pair, to_other), sides(cnt)):
        out[...] = message[part(side, MESSAGE), :]
    copies[7].wait()


def own_kernel(wt, dirs, blocks, face_blocks, weighted, matrices, faces, blk_f):
    for k in range(FACES):
        faces[:, k * P_SIZE : (k + 1) * P_SIZE] = -face_blocks[k]
    weight = wt[...]
    for s in range(E_DEV):
        weighted[rows(s), :] = (wide_column(weight, s) * dirs[rows(s), :].astype(F32)).astype(BF16)
    for g in range(E_DEV // 16):
        for c in range(HALF):
            x = blocks[g * 16 : (g + 1) * 16, c * NV : (c + 1) * NV].astype(F32)
            for p in range(2):
                blk_f[pl.ds(2 * c + p, 16, stride=P_SIZE + 1), :] = jnp.where(lane_is(p), x, 0.0)
        for e in range(16):
            matrices[rows(g * 16 + e), :] = blk_f[pl.ds(e * (P_SIZE + 1), P_SIZE), :].astype(BF16)


ARRIVED = MESSAGE - DIR_AT
BLK_IN = BLK_AT - DIR_AT
SOIL_IN = SOIL_AT - DIR_AT


def arrive_kernel(other, pair, cnt, cap_own, wt_own, own, to_above, to_below, came, cap_out, wt_out, moved, soil_f):
    mine_left, mine_right, arrive_left, arrive_right, live = moves(cnt)
    for ref, side in zip((pair, other), sides(cnt)):
        came[part(side, ARRIVED), :] = ref[DIR_AT:, :]
    soil_f[...] = jnp.full((2 * NV, NV), 1.0, F32)
    for side in range(2):
        x = came[pl.ds(side * ARRIVED + SOIL_IN, 2 * MIG), :].astype(F32)
        for k in range(2):
            soil_f[k * NV + side * MIG : k * NV + (side + 1) * MIG, :] = x[k * MIG : (k + 1) * MIG]
    capacity, weight = closures_by_column(soil_f[...])
    lane = lax.broadcasted_iota(jnp.int32, (P_SIZE, NV), 1)
    for out, mine, theirs in ((cap_out, cap_own, capacity), (wt_out, wt_own, weight)):
        middle = pltpu.roll(mine[...], lax.rem(arrive_left - mine_left + NV, NV), 1)
        left = pltpu.roll(theirs, lax.rem(arrive_left - MIG + NV, NV), 1)
        right = pltpu.roll(theirs, E_BAL - arrive_right - MIG, 1)
        out[...] = jnp.where(lane < arrive_left, left, jnp.where(lane < E_BAL - arrive_right, middle, right))
    for i in range(2 * MIG):
        raw = came[rows(i % MIG, base=i // MIG * ARRIVED), :]
        moved[rows(i), :] = (wide_column(weight, i) * raw.astype(F32)).astype(BF16)
    shift = mine_left - arrive_left
    for i in range(LAYER):
        here = own[rows(jnp.maximum(shift + i, 0)), :].astype(F32)
        came = moved[rows(jnp.minimum(MIG - arrive_left + i, MIG - 1)), :].astype(F32)
        to_above[rows(i), :] = jnp.where(i < arrive_left, came, here).astype(BF16)
        w = E_BAL - LAYER + i
        here = own[rows(shift + w), :].astype(F32)
        came = moved[rows(jnp.maximum(w - E_BAL + arrive_right, 0) + MIG), :].astype(F32)
        to_below[rows(i), :] = jnp.where(w >= E_BAL - arrive_right, came, here).astype(BF16)


def first_kernel(
    cnt, nbr, cap, wt, faces, dirs, own, matrices, came, above, below, pair, other,
    blk_out, partial, first, nxt, near, blk_f,
):
    mine_left, mine_right, arrive_left, arrive_right, live = moves(cnt)
    shift = mine_left - arrive_left
    for w in range(E_BAL):
        if w < LAYER:
            near[rows(w), :] = above[rows(w), :]
        elif w >= E_BAL - LAYER:
            near[rows(w), :] = below[rows(w - E_BAL + LAYER), :]
        else:
            near[rows(w), :] = own[rows(shift + w), :]
    for ref, side in zip((pair, other), sides(cnt)):
        at = pl.multiple_of((E_BAL + side * RIM) * P_SIZE, P_SIZE)
        near[pl.ds(at, RIM * P_SIZE), :] = ref[0 : RIM * P_SIZE, :]
    for i in range(MIG):

        @pl.when(i < mine_left)
        def _():
            near[rows(E_BAL + RIM - mine_left + i), :] = own[rows(i), :]

        @pl.when(i < mine_right)
        def _():
            near[rows(E_BAL + RIM + i), :] = own[rows(live - mine_right + i), :]

    near[rows(ABOVE), :] = jnp.zeros((P_SIZE, NV), BF16)

    for w in range(E_BAL):
        blk_out[rows(w), :] = matrices[rows(jnp.maximum(shift + w, 0)), :]
    for i in range(MIG):

        @pl.when(i < arrive_left)
        def _():
            x = came[rows(MIG - arrive_left + i, HALF, BLK_IN), :].astype(F32)
            for p in range(2):
                blk_f[pl.ds(p, HALF, stride=2), :] = jnp.where(lane_is(p), x, 0.0)
            blk_out[rows(i), :] = blk_f[...].astype(BF16)

        @pl.when(i < arrive_right)
        def _():
            x = came[rows(i, HALF, ARRIVED + BLK_IN), :].astype(F32)
            for p in range(2):
                blk_f[pl.ds(p, HALF, stride=2), :] = jnp.where(lane_is(p), x, 0.0)
            blk_out[rows(E_BAL - arrive_right + i), :] = blk_f[...].astype(BF16)

    capacity = cap[...]
    weight = wt[...]
    face_rows = faces[...]
    for w in range(E_BAL):
        vector = dirs[rows(jnp.maximum(shift + w, 0)), :].astype(F32)
        if w < MIG:
            arrived = came[rows(jnp.minimum(MIG - arrive_left + w, MIG - 1)), :].astype(F32)
            vector = jnp.where(w < arrive_left, arrived, vector)
        elif w >= E_BAL - MIG:
            arrived = came[rows(jnp.maximum(w - E_BAL + arrive_right, 0), base=ARRIVED), :].astype(F32)
            vector = jnp.where(w >= E_BAL - arrive_right, arrived, vector)
        result = wide_column(capacity, w) * vector + product(near, nbr, blk_out, face_rows, w, ABOVE, ABOVE)
        if LAYER <= w < E_BAL - LAYER:
            rounded = result.astype(BF16)
            first[rows(w - LAYER), :] = rounded
            nxt[rows(w - LAYER), :] = (wide_column(weight, w) * rounded.astype(F32)).astype(BF16)
        else:
            partial[rows(w if w < LAYER else w - E_BAL + 2 * LAYER), :] = result


def product(near, nbr, matrices, face_rows, w, limit, missing):
    mine = near[rows(w), :]
    parts = [mine, mine]
    for k in range(FACES):
        b = nbr[k, 0, w]
        b = jnp.where((b < 0) | (b >= limit), missing, b)
        parts.append(near[rows(b), :])
    lhs = jnp.concatenate([matrices[rows(w), :], face_rows], 1)
    return jnp.dot(lhs, jnp.concatenate(parts, 0), preferred_element_type=F32)


def vertical(nbr, faces, from_above, from_below, i):
    top = i < LAYER
    w = i if top else E_BAL - 2 * LAYER + i
    k = 4 if top else 5
    came = from_above if top else from_below
    inside = nbr[k, 0, w] - (ABOVE if top else BELOW)
    there = (inside >= 0) & (inside < LAYER)
    row = came[rows(jnp.clip(inside, 0, LAYER - 1)), :]
    update = jnp.dot(faces[:, k * P_SIZE : (k + 1) * P_SIZE], row, preferred_element_type=F32)
    return w, jnp.where(there, update, 0.0)


def ends_kernel(
    cnt, nbr, wt, faces, partial, from_above, from_below, nxt, first, to_other, to_pair, to_above, to_below, near, rim,
):
    weight = wt[...]
    for i in range(2 * LAYER):
        w, update = vertical(nbr, faces, from_above, from_below, i)
        rounded = (partial[rows(i), :] + update).astype(BF16)
        first[rows(i), :] = rounded
        onward = (wide_column(weight, w) * rounded.astype(F32)).astype(BF16)
        if i < LAYER:
            rim[rows(i), :] = onward
            to_above[rows(i), :] = onward
        else:
            rim[rows(RIM + i), :] = onward
            to_below[rows(i - LAYER), :] = onward
    span = LAYER * P_SIZE
    rim[span : 3 * span, :] = jnp.concatenate(
        [nxt[0:span, :], nxt[(E_BAL - 3 * LAYER) * P_SIZE : (E_BAL - 2 * LAYER) * P_SIZE, :]], 0
    )
    for out, side in zip((to_pair, to_other), sides(cnt)):
        out[...] = rim[part(side, RIM * P_SIZE), :]
    near[0:span, :] = rim[0:span, :]
    near[span : (E_BAL - LAYER) * P_SIZE, :] = nxt[...]
    near[(E_BAL - LAYER) * P_SIZE :, :] = rim[3 * span :, :]


def second_kernel(other, pair, cnt, nbr, cap, faces, matrices, mid, ends, own, out, partial, near, done, sems):
    near[0 : E_BAL * P_SIZE, :] = own[...]
    for ref, side in zip((pair, other), sides(cnt)):
        at = pl.multiple_of((E_BAL + side * RIM) * P_SIZE, P_SIZE)
        near[pl.ds(at, RIM * P_SIZE), :] = ref[...]
    near[rows(ABOVE), :] = jnp.zeros((P_SIZE, NV), BF16)
    capacity = cap[...]
    face_rows = faces[...]
    copies = []
    for w in range(E_BAL):
        outer = w if w < LAYER else w - E_BAL + 2 * LAYER
        inner = LAYER <= w < E_BAL - LAYER
        vector = mid[rows(w - LAYER), :] if inner else ends[rows(outer), :]
        result = wide_column(capacity, w) * vector.astype(F32) + product(
            near, nbr, matrices, face_rows, w, ABOVE, ABOVE
        )
        if inner:
            done[rows(w - LAYER), :] = result.astype(BF16)
            if (w - LAYER) % PIECE == PIECE - 1:
                span = (w - LAYER + 1 - PIECE) * P_SIZE
                copies.append(
                    pltpu.make_async_copy(
                        done.at[pl.ds(span, PIECE * P_SIZE)],
                        out.at[pl.ds(span + LAYER * P_SIZE, PIECE * P_SIZE)],
                        sems.at[len(copies)],
                    )
                )
                copies[-1].start()
        else:
            partial[rows(outer), :] = result
    for copy in copies:
        copy.wait()


PIECE = 16


def finish_kernel(nbr, faces, partial, from_above, from_below, begun, out, done, sems):
    copies = []
    for i in range(2 * LAYER):
        w, update = vertical(nbr, faces, from_above, from_below, i)
        done[rows(i), :] = (partial[rows(i), :] + update).astype(BF16)
        if i % LAYER == LAYER - 1:
            span = LAYER * P_SIZE
            copies.append(
                pltpu.make_async_copy(
                    done.at[pl.ds((i + 1) * P_SIZE - span, span)],
                    out.at[pl.ds((w + 1) * P_SIZE - span, span)],
                    sems.at[len(copies)],
                )
            )
            copies[-1].start()
    for copy in copies:
        copy.wait()


def smem():
    return pl.BlockSpec(memory_space=pltpu.SMEM)


def vmem():
    return pl.BlockSpec(memory_space=pltpu.VMEM)


def hbm():
    return pl.BlockSpec(memory_space=pltpu.HBM)


def pinned(x):
    return pltpu.with_memory_space_constraint(x, pltpu.HBM)


def held(n, kind=BF16):
    return pltpu.VMEM((n, NV), kind)


def call(kernel, name, ins, arrays, outs, out_specs=None, scratch=(), flops=0, moved=0, aliases=None):
    return pl.pallas_call(
        kernel,
        out_shape=outs,
        in_specs=ins,
        out_specs=out_specs or [vmem()] * len(outs),
        scratch_shapes=list(scratch),
        compiler_params=pltpu.CompilerParams(vmem_limit_bytes=20 * 2**20),
        cost_estimate=pl.CostEstimate(flops=flops, bytes_accessed=moved, transcendentals=0),
        input_output_aliases=aliases or {},
        name=name,
    )(*arrays)


def shifted(value, axis, by):
    peers = lax.axis_size(axis)
    return lax.ppermute(value, axis, [(i, (i + by) % peers) for i in range(peers)])


def swapped(value, first):
    pairs = []
    for t in range(N_WIDE):
        partner = t + 1 if (t - first) % 2 == 0 else t - 1
        for c in range(COLS):
            target = (partner, c) if 0 <= partner < N_WIDE else (t, c ^ 1)
            pairs.append((t * COLS + c, target[0] * COLS + target[1]))
    return lax.ppermute(value, ("wide", "narrow"), pairs)


def per_device(soil_state, directions, blocks, send_left, send_right, neighbours, face_blocks):
    soil = soil_state[0]
    dirs = directions.reshape(E_DEV * P_SIZE, NV)
    rows_of = blocks[0]
    column = held(P_SIZE, F32)
    layer, rim = held(LAYER * P_SIZE), held(RIM * P_SIZE)
    slots = held(E_DEV * P_SIZE)
    inner = held((E_BAL - 2 * LAYER) * P_SIZE)

    to_other, to_pair, cap_own, wt_own, cnt, nbr = call(
        prepare_kernel, "prepare", [hbm()] * 6,
        [pinned(x) for x in (send_left, send_right, jnp.swapaxes(neighbours, 0, 1), soil, dirs, rows_of)],
        (held(MESSAGE), held(MESSAGE), column, column, pltpu.SMEM((PARITY + 1,), jnp.int32), pltpu.SMEM((FACES, 1, E_BAL), jnp.int32)),
        [vmem()] * 4 + [smem()] * 2,
        (
            pltpu.SMEM((N_WIDE,), jnp.int32), pltpu.SMEM((N_WIDE,), jnp.int32),
            pltpu.VMEM((E_DEV, 2 * NV), BF16), pltpu.VMEM((2 * NV, NV), F32),
            pltpu.VMEM((HEAD * P_SIZE, NV), BF16), pltpu.VMEM((TAIL * P_SIZE, NV), BF16),
            pltpu.VMEM((16, P_SIZE * P_SIZE), BF16), pltpu.VMEM((BLK_TAIL, P_SIZE * P_SIZE), BF16),
            held(48 * PITCH, F32), held(2 * MESSAGE), pltpu.SemaphoreType.DMA((8,)),
        ),
    )
    other = swapped(to_other, 1)
    pair = swapped(to_pair, 0)

    own, matrices, faces = call(
        own_kernel, "own", [vmem()] * 4, (wt_own, dirs, rows_of, face_blocks),
        (slots, slots, pltpu.VMEM((P_SIZE, FACES * P_SIZE), BF16)),
        scratch=(held(16 * (P_SIZE + 1), F32),),
        flops=10**9, moved=6 * 2**20,
    )

    above, below, came, cap, wt = call(
        arrive_kernel, "arrive", [vmem()] * 2 + [smem()] + [vmem()] * 3, (other, pair, cnt, cap_own, wt_own, own),
        (layer, layer, held(2 * ARRIVED), column, column),
        scratch=(held(2 * MIG * P_SIZE), pltpu.VMEM((2 * NV, NV), F32)),
    )
    from_below = shifted(above, "narrow", -1)
    from_above = shifted(below, "narrow", 1)

    blk, partial, first, nxt = call(
        first_kernel, "first", [smem()] * 2 + [vmem()] * 11,
        (cnt, nbr, cap, wt, faces, dirs, own, matrices, came, above, below, pair, other),
        (held(E_BAL * P_SIZE), held(2 * LAYER * P_SIZE, F32), inner, inner),
        scratch=(held((ABOVE + 1) * P_SIZE), held(P_SIZE, F32)),
        flops=2 * 10**9, moved=8 * 2**20,
    )
    ends, go_other, go_pair, go_above, go_below, onward = call(
        ends_kernel, "ends", [smem()] * 2 + [vmem()] * 6, (cnt, nbr, wt, faces, partial, from_above, from_below, nxt),
        (held(2 * LAYER * P_SIZE), rim, rim, layer, layer, held(E_BAL * P_SIZE)),
        scratch=(held(2 * RIM * P_SIZE),),
    )
    other = swapped(go_other, 1)
    pair = swapped(go_pair, 0)
    came_below = shifted(go_above, "narrow", -1)
    came_above = shifted(go_below, "narrow", 1)
    result = jax.ShapeDtypeStruct((E_BAL * P_SIZE, NV), BF16)
    begun, partial = call(
        second_kernel, "second", [vmem()] * 2 + [smem()] * 2 + [vmem()] * 6,
        (other, pair, cnt, nbr, cap, faces, blk, first, ends, onward),
        (result, held(2 * LAYER * P_SIZE, F32)), [hbm(), vmem()],
        scratch=(
            held((ABOVE + 1) * P_SIZE), held((E_BAL - 2 * LAYER) * P_SIZE),
            pltpu.SemaphoreType.DMA(((E_BAL - 2 * LAYER) // PIECE,)),
        ),
        flops=10**9, moved=6 * 2**20,
    )
    (out,) = call(
        finish_kernel, "finish", [smem()] + [vmem()] * 4 + [hbm()],
        (nbr, faces, partial, came_above, came_below, begun),
        (result,), [hbm()],
        scratch=(held(2 * LAYER * P_SIZE), pltpu.SemaphoreType.DMA((2,))),
        aliases={5: 0},
    )
    return out.reshape(1, E_BAL, P_SIZE, NV)


def solution(mesh):
    in_specs = (
        P("narrow", "wide", None),
        P("narrow", "wide", None, None),
        P("narrow", "wide", None),
        P(),
        P(),
        P("narrow", None, "wide"),
        P(),
    )
    out_specs = P("narrow", "wide", None, None)
    return jax.shard_map(
        per_device, mesh=mesh, in_specs=in_specs, out_specs=out_specs, check_vma=False
    )
```

```python
import jax
import jax.numpy as jnp
from jax import lax
from jax.experimental import pallas as pl
from jax.experimental.pallas import tpu as pltpu
from jax.sharding import PartitionSpec as P

P_SIZE = 64
FACES = 6
NV = 128
E_BAL = 64
MIG = 8
RIM = 16
LAYER = 8
E_DEV = 80
N_WIDE = 64
COLS = 4
HALF = P_SIZE // 2
ABOVE = E_BAL + 2 * RIM
BELOW = ABOVE + LAYER
MISSING = BELOW + LAYER

DIR_AT = RIM * P_SIZE
BLK_AT = DIR_AT + MIG * P_SIZE
SOIL_AT = BLK_AT + MIG * HALF
MESSAGE = SOIL_AT + 2 * MIG

moisture_range = 0.4
time_step = 0.5

F32 = jnp.float32
BF16 = jnp.bfloat16


def closures(pressure, inverse_entry, pore_index, conduct_sat):
    exponent = 1.0 - 1.0 / pore_index
    log_scaled = jnp.log(-inverse_entry * pressure)
    power = jnp.exp(pore_index * log_scaled)
    log_denom = jnp.log1p(power)
    saturation = jnp.exp(-exponent * log_denom)
    ratio_log = pore_index * log_scaled - log_denom
    relative = jnp.sqrt(saturation) * jnp.square(1.0 - jnp.exp(exponent * ratio_log))
    capacity = (
        moisture_range
        * inverse_entry
        * pore_index
        * exponent
        * jnp.exp((pore_index - 1.0) * log_scaled - (exponent + 1.0) * log_denom)
        / time_step
    )
    return capacity, conduct_sat * relative


def closures_by_column(soil_rows):
    cols = [jnp.transpose(soil_rows[k * NV : (k + 1) * NV]) for k in range(2)]
    fields = [cols[i // 2][i % 2 * P_SIZE : (i % 2 + 1) * P_SIZE] for i in range(4)]
    return closures(*fields)


def counts(send_left, send_right):
    t = lax.axis_index("wide")
    before = lax.rem(t + N_WIDE - 1, N_WIDE)
    after = lax.rem(t + 1, N_WIDE)
    mine_left = send_left[t]
    mine_right = send_right[t]
    arrive_left = jnp.where(t > 0, send_right[before], 0)
    arrive_right = jnp.where(t < N_WIDE - 1, send_left[after], 0)
    return mine_left, mine_right, arrive_left, arrive_right


PARITY = 4


def sides(cnt):
    return 1 - cnt[PARITY], cnt[PARITY]


def part(side, size):
    return pl.ds(pl.multiple_of(side * size, size if size % 16 == 0 else 16), size)


def moves(cnt):
    mine_left, mine_right, arrive_left, arrive_right = (cnt[i] for i in range(4))
    live = E_BAL + mine_left + mine_right - arrive_left - arrive_right
    return mine_left, mine_right, arrive_left, arrive_right, live


def rows(index, size=P_SIZE, base=0):
    if isinstance(index, int):
        return pl.ds(base + index * size, size)
    return pl.ds(pl.multiple_of(base + index * size, 16), size)


def wide_column(columns, lane):
    return jnp.broadcast_to(columns[:, lane : lane + 1], (P_SIZE, NV))


def lane_is(p):
    return (lax.broadcasted_iota(jnp.int32, (1, NV), 1) >= P_SIZE) == bool(p)


PITCH = HALF + 1
HEAD = MIG + RIM
TAIL = E_DEV - 40
BLK_TAIL = E_DEV - 32


def prepare_kernel(
    sl, sr, nbr, soil, dirs, blocks, to_other, to_pair, cap_out, wt_out, cnt, nbr_out,
    sl_s, sr_s, soil_b, soil_f, dir_head, dir_tail, blk_head, blk_tail, blk_f, message, sems,
):
    to_left = message.at[pl.ds(0, MESSAGE)]
    to_right = message.at[pl.ds(MESSAGE, MESSAGE)]
    copies = [
        pltpu.make_async_copy(source, target, sems.at[i])
        for i, (source, target) in enumerate((
            (soil, soil_b),
            (sl, sl_s),
            (sr, sr_s),
            (dirs.at[pl.ds(0, HEAD * P_SIZE)], dir_head),
            (dirs.at[pl.ds((E_DEV - TAIL) * P_SIZE, TAIL * P_SIZE)], dir_tail),
            (blocks.at[pl.ds(0, 16)], blk_head),
            (blocks.at[pl.ds(E_DEV - BLK_TAIL, BLK_TAIL)], blk_tail),
            (nbr, nbr_out),
        ))
    ]
    for copy in copies:
        copy.start()
    for k in range(2):
        soil_f[k * NV + E_DEV : (k + 1) * NV, :] = jnp.full((NV - E_DEV, NV), 1.0, F32)
    copies[0].wait()
    for k in range(2):
        soil_f[k * NV : k * NV + E_DEV, :] = soil_b[:, k * NV : (k + 1) * NV].astype(F32)
    capacity, weight = closures_by_column(soil_f[...])
    wt_out[...] = weight
    cap_out[...] = capacity
    copies[1].wait()
    copies[2].wait()
    for i, n in enumerate(counts(sl_s, sr_s)):
        cnt[i] = n
    cnt[PARITY] = lax.rem(lax.axis_index("wide"), 2)
    mine_left, mine_right, arrive_left, arrive_right, live = moves(cnt)
    middle = mine_left - arrive_left
    tail = live - MIG
    here = pltpu.roll(weight, lax.rem(NV - middle, NV), 1)
    copies[3].wait()
    copies[4].wait()
    for i in range(RIM):
        s = middle + E_BAL - RIM + i - (E_DEV - TAIL)
        to_right[rows(i), :] = (wide_column(here, E_BAL - RIM + i) * dir_tail[rows(s), :].astype(F32)).astype(BF16)
        s = jnp.maximum(middle + i, 0)
        to_left[rows(i), :] = (wide_column(here, i) * dir_head[rows(s), :].astype(F32)).astype(BF16)
    at = pl.multiple_of((tail - (E_DEV - TAIL)) * P_SIZE, P_SIZE)
    to_right[pl.ds(DIR_AT, MIG * P_SIZE), :] = dir_tail[pl.ds(at, MIG * P_SIZE), :]
    to_left[pl.ds(DIR_AT, MIG * P_SIZE), :] = dir_head[0 : MIG * P_SIZE, :]
    for out, first in ((to_right, tail), (to_left, 0)):
        both = jnp.concatenate([soil_f[pl.ds(k * NV + first, MIG), :] for k in range(2)], 0)
        out[pl.ds(SOIL_AT, 2 * MIG), :] = both.astype(BF16)
    copies[5].wait()
    copies[6].wait()
    start = E_DEV - BLK_TAIL
    group = jnp.minimum(lax.div(tail - start, 16) * 16, BLK_TAIL - 32)
    for g in range(3):
        for c in range(HALF):
            lanes = slice(c * NV, (c + 1) * NV)
            if g == 0:
                x = blk_head[:, lanes]
            else:
                x = blk_tail[pl.ds(pl.multiple_of(group + 16 * (g - 1), 16), 16), lanes]
            blk_f[pl.ds(g * 16 * PITCH + c, 16, stride=PITCH), :] = x.astype(F32)
    for i in range(MIG):
        at = (16 + tail - start - group + i) * PITCH
        to_right[rows(i, HALF, BLK_AT), :] = blk_f[pl.ds(at, HALF), :].astype(BF16)
        to_left[rows(i, HALF, BLK_AT), :] = blk_f[pl.ds(i * PITCH, HALF), :].astype(BF16)
    for out, side in zip((to_pair, to_other), sides(cnt)):
        out[...] = message[part(side, MESSAGE), :]
    copies[7].wait()


def own_kernel(wt, dirs, blocks, face_blocks, weighted, matrices, faces, blk_f):
    for k in range(FACES):
        faces[:, k * P_SIZE : (k + 1) * P_SIZE] = -face_blocks[k]
    weight = wt[...]
    for s in range(E_DEV):
        weighted[rows(s), :] = (wide_column(weight, s) * dirs[rows(s), :].astype(F32)).astype(BF16)
    for g in range(E_DEV // 16):
        for c in range(HALF):
            x = blocks[g * 16 : (g + 1) * 16, c * NV : (c + 1) * NV].astype(F32)
            for p in range(2):
                blk_f[pl.ds(2 * c + p, 16, stride=P_SIZE + 1), :] = jnp.where(lane_is(p), x, 0.0)
        for e in range(16):
            matrices[rows(g * 16 + e), :] = blk_f[pl.ds(e * (P_SIZE + 1), P_SIZE), :].astype(BF16)


ARRIVED = MESSAGE - DIR_AT
BLK_IN = BLK_AT - DIR_AT
SOIL_IN = SOIL_AT - DIR_AT


def arrive_kernel(other, pair, cnt, cap_own, wt_own, own, to_above, to_below, came, cap_out, wt_out, moved, soil_f):
    mine_left, mine_right, arrive_left, arrive_right, live = moves(cnt)
    for ref, side in zip((pair, other), sides(cnt)):
        came[part(side, ARRIVED), :] = ref[DIR_AT:, :]
    soil_f[...] = jnp.full((2 * NV, NV), 1.0, F32)
    for side in range(2):
        x = came[pl.ds(side * ARRIVED + SOIL_IN, 2 * MIG), :].astype(F32)
        for k in range(2):
            soil_f[k * NV + side * MIG : k * NV + (side + 1) * MIG, :] = x[k * MIG : (k + 1) * MIG]
    capacity, weight = closures_by_column(soil_f[...])
    lane = lax.broadcasted_iota(jnp.int32, (P_SIZE, NV), 1)
    for out, mine, theirs in ((cap_out, cap_own, capacity), (wt_out, wt_own, weight)):
        middle = pltpu.roll(mine[...], lax.rem(arrive_left - mine_left + NV, NV), 1)
        left = pltpu.roll(theirs, lax.rem(arrive_left - MIG + NV, NV), 1)
        right = pltpu.roll(theirs, E_BAL - arrive_right - MIG, 1)
        out[...] = jnp.where(lane < arrive_left, left, jnp.where(lane < E_BAL - arrive_right, middle, right))
    for i in range(2 * MIG):
        raw = came[rows(i % MIG, base=i // MIG * ARRIVED), :]
        moved[rows(i), :] = (wide_column(weight, i) * raw.astype(F32)).astype(BF16)
    shift = mine_left - arrive_left
    for i in range(LAYER):
        here = own[rows(jnp.maximum(shift + i, 0)), :].astype(F32)
        came = moved[rows(jnp.minimum(MIG - arrive_left + i, MIG - 1)), :].astype(F32)
        to_above[rows(i), :] = jnp.where(i < arrive_left, came, here).astype(BF16)
        w = E_BAL - LAYER + i
        here = own[rows(shift + w), :].astype(F32)
        came = moved[rows(jnp.maximum(w - E_BAL + arrive_right, 0) + MIG), :].astype(F32)
        to_below[rows(i), :] = jnp.where(w >= E_BAL - arrive_right, came, here).astype(BF16)


def first_kernel(
    cnt, nbr, cap, wt, faces, dirs, own, matrices, came, above, below, pair, other,
    blk_out, partial, first, nxt, near, blk_f,
):
    mine_left, mine_right, arrive_left, arrive_right, live = moves(cnt)
    shift = mine_left - arrive_left
    for w in range(E_BAL):
        if w < LAYER:
            near[rows(w), :] = above[rows(w), :]
        elif w >= E_BAL - LAYER:
            near[rows(w), :] = below[rows(w - E_BAL + LAYER), :]
        else:
            near[rows(w), :] = own[rows(shift + w), :]
    for ref, side in zip((pair, other), sides(cnt)):
        at = pl.multiple_of((E_BAL + side * RIM) * P_SIZE, P_SIZE)
        near[pl.ds(at, RIM * P_SIZE), :] = ref[0 : RIM * P_SIZE, :]
    for i in range(MIG):

        @pl.when(i < mine_left)
        def _():
            near[rows(E_BAL + RIM - mine_left + i), :] = own[rows(i), :]

        @pl.when(i < mine_right)
        def _():
            near[rows(E_BAL + RIM + i), :] = own[rows(live - mine_right + i), :]

    near[rows(ABOVE), :] = jnp.zeros((P_SIZE, NV), BF16)

    for w in range(E_BAL):
        blk_out[rows(w), :] = matrices[rows(jnp.maximum(shift + w, 0)), :]
    for i in range(MIG):

        @pl.when(i < arrive_left)
        def _():
            x = came[rows(MIG - arrive_left + i, HALF, BLK_IN), :].astype(F32)
            for p in range(2):
                blk_f[pl.ds(p, HALF, stride=2), :] = jnp.where(lane_is(p), x, 0.0)
            blk_out[rows(i), :] = blk_f[...].astype(BF16)

        @pl.when(i < arrive_right)
        def _():
            x = came[rows(i, HALF, ARRIVED + BLK_IN), :].astype(F32)
            for p in range(2):
                blk_f[pl.ds(p, HALF, stride=2), :] = jnp.where(lane_is(p), x, 0.0)
            blk_out[rows(E_BAL - arrive_right + i), :] = blk_f[...].astype(BF16)

    capacity = cap[...]
    weight = wt[...]
    face_rows = faces[...]
    for w in range(E_BAL):
        vector = dirs[rows(jnp.maximum(shift + w, 0)), :].astype(F32)
        if w < MIG:
            arrived = came[rows(jnp.minimum(MIG - arrive_left + w, MIG - 1)), :].astype(F32)
            vector = jnp.where(w < arrive_left, arrived, vector)
        elif w >= E_BAL - MIG:
            arrived = came[rows(jnp.maximum(w - E_BAL + arrive_right, 0), base=ARRIVED), :].astype(F32)
            vector = jnp.where(w >= E_BAL - arrive_right, arrived, vector)
        result = wide_column(capacity, w) * vector + product(near, nbr, blk_out, face_rows, w, ABOVE, ABOVE)
        if LAYER <= w < E_BAL - LAYER:
            rounded = result.astype(BF16)
            first[rows(w - LAYER), :] = rounded
            nxt[rows(w - LAYER), :] = (wide_column(weight, w) * rounded.astype(F32)).astype(BF16)
        else:
            partial[rows(w if w < LAYER else w - E_BAL + 2 * LAYER), :] = result


def product(near, nbr, matrices, face_rows, w, limit, missing):
    mine = near[rows(w), :]
    parts = [mine, mine]
    for k in range(FACES):
        b = nbr[k, 0, w]
        b = jnp.where((b < 0) | (b >= limit), missing, b)
        parts.append(near[rows(b), :])
    lhs = jnp.concatenate([matrices[rows(w), :], face_rows], 1)
    return jnp.dot(lhs, jnp.concatenate(parts, 0), preferred_element_type=F32)


def vertical(nbr, faces, from_above, from_below, i):
    top = i < LAYER
    w = i if top else E_BAL - 2 * LAYER + i
    k = 4 if top else 5
    came = from_above if top else from_below
    inside = nbr[k, 0, w] - (ABOVE if top else BELOW)
    there = (inside >= 0) & (inside < LAYER)
    row = came[rows(jnp.clip(inside, 0, LAYER - 1)), :]
    update = jnp.dot(faces[:, k * P_SIZE : (k + 1) * P_SIZE], row, preferred_element_type=F32)
    return w, jnp.where(there, update, 0.0)


def ends_kernel(
    cnt, nbr, wt, faces, partial, from_above, from_below, nxt, first, to_other, to_pair, to_above, to_below, near, rim,
):
    weight = wt[...]
    for i in range(2 * LAYER):
        w, update = vertical(nbr, faces, from_above, from_below, i)
        rounded = (partial[rows(i), :] + update).astype(BF16)
        first[rows(i), :] = rounded
        onward = (wide_column(weight, w) * rounded.astype(F32)).astype(BF16)
        if i < LAYER:
            rim[rows(i), :] = onward
            to_above[rows(i), :] = onward
        else:
            rim[rows(RIM + i), :] = onward
            to_below[rows(i - LAYER), :] = onward
    span = LAYER * P_SIZE
    rim[span : 3 * span, :] = jnp.concatenate(
        [nxt[0:span, :], nxt[(E_BAL - 3 * LAYER) * P_SIZE : (E_BAL - 2 * LAYER) * P_SIZE, :]], 0
    )
    for out, side in zip((to_pair, to_other), sides(cnt)):
        out[...] = rim[part(side, RIM * P_SIZE), :]
    near[0:span, :] = rim[0:span, :]
    near[span : (E_BAL - LAYER) * P_SIZE, :] = nxt[...]
    near[(E_BAL - LAYER) * P_SIZE :, :] = rim[3 * span :, :]


def inner_kernel(pair, cnt, nbr, cap, faces, matrices, mid, ends, own, partial, near):
    near[0 : E_BAL * P_SIZE, :] = own[...]
    here, there = sides(cnt)
    at = pl.multiple_of((E_BAL + here * RIM) * P_SIZE, P_SIZE)
    near[pl.ds(at, RIM * P_SIZE), :] = pair[...]
    at = pl.multiple_of((E_BAL + there * RIM) * P_SIZE, P_SIZE)
    near[pl.ds(at, RIM * P_SIZE), :] = jnp.zeros((RIM * P_SIZE, NV), BF16)
    near[rows(ABOVE), :] = jnp.zeros((P_SIZE, NV), BF16)
    capacity = cap[...]
    face_rows = faces[...]
    for w in range(E_BAL):
        outer = w if w < LAYER else w - E_BAL + 2 * LAYER
        inner = LAYER <= w < E_BAL - LAYER
        vector = mid[rows(w - LAYER), :] if inner else ends[rows(outer), :]
        partial[rows(w), :] = wide_column(capacity, w) * vector.astype(F32) + product(
            near, nbr, matrices, face_rows, w, ABOVE, ABOVE
        )


PIECE = 8


def second_kernel(other, cnt, nbr, faces, inside, from_above, from_below, out, near, done, sems):
    near[0 : RIM * P_SIZE, :] = other[...]
    near[rows(RIM), :] = jnp.zeros((P_SIZE, NV), BF16)
    first = E_BAL + sides(cnt)[1] * RIM
    sideways = faces[:, 0 : 4 * P_SIZE]
    copies = []
    for w in range(E_BAL):
        parts = []
        for k in range(4):
            b = nbr[k, 0, w] - first
            parts.append(near[rows(jnp.where((b < 0) | (b >= RIM), RIM, b)), :])
        result = inside[rows(w), :] + jnp.dot(
            sideways, jnp.concatenate(parts, 0), preferred_element_type=F32
        )
        if w < LAYER or w >= E_BAL - LAYER:
            i = w if w < LAYER else w - E_BAL + 2 * LAYER
            result = result + vertical(nbr, faces, from_above, from_below, i)[1]
        done[rows(w), :] = result.astype(BF16)
        if w % PIECE == PIECE - 1:
            span = pl.ds((w + 1 - PIECE) * P_SIZE, PIECE * P_SIZE)
            copies.append(pltpu.make_async_copy(done.at[span], out.at[span], sems.at[len(copies)]))
            copies[-1].start()
    for copy in copies:
        copy.wait()


def smem():
    return pl.BlockSpec(memory_space=pltpu.SMEM)


def vmem():
    return pl.BlockSpec(memory_space=pltpu.VMEM)


def hbm():
    return pl.BlockSpec(memory_space=pltpu.HBM)


def pinned(x):
    return pltpu.with_memory_space_constraint(x, pltpu.HBM)


def held(n, kind=BF16):
    return pltpu.VMEM((n, NV), kind)


def call(kernel, name, ins, arrays, outs, out_specs=None, scratch=(), flops=0, moved=0, aliases=None):
    return pl.pallas_call(
        kernel,
        out_shape=outs,
        in_specs=ins,
        out_specs=out_specs or [vmem()] * len(outs),
        scratch_shapes=list(scratch),
        compiler_params=pltpu.CompilerParams(vmem_limit_bytes=20 * 2**20),
        cost_estimate=pl.CostEstimate(flops=flops, bytes_accessed=moved, transcendentals=0),
        input_output_aliases=aliases or {},
        name=name,
    )(*arrays)


def shifted(value, axis, by):
    peers = lax.axis_size(axis)
    return lax.ppermute(value, axis, [(i, (i + by) % peers) for i in range(peers)])


def swapped(value, first):
    pairs = []
    for t in range(N_WIDE):
        partner = t + 1 if (t - first) % 2 == 0 else t - 1
        for c in range(COLS):
            target = (partner, c) if 0 <= partner < N_WIDE else (t, c ^ 1)
            pairs.append((t * COLS + c, target[0] * COLS + target[1]))
    return lax.ppermute(value, ("wide", "narrow"), pairs)


def per_device(soil_state, directions, blocks, send_left, send_right, neighbours, face_blocks):
    soil = soil_state[0]
    dirs = directions.reshape(E_DEV * P_SIZE, NV)
    rows_of = blocks[0]
    column = held(P_SIZE, F32)
    layer, rim = held(LAYER * P_SIZE), held(RIM * P_SIZE)
    slots = held(E_DEV * P_SIZE)
    inner = held((E_BAL - 2 * LAYER) * P_SIZE)

    to_other, to_pair, cap_own, wt_own, cnt, nbr = call(
        prepare_kernel, "prepare", [hbm()] * 6,
        [pinned(x) for x in (send_left, send_right, jnp.swapaxes(neighbours, 0, 1), soil, dirs, rows_of)],
        (held(MESSAGE), held(MESSAGE), column, column, pltpu.SMEM((PARITY + 1,), jnp.int32), pltpu.SMEM((FACES, 1, E_BAL), jnp.int32)),
        [vmem()] * 4 + [smem()] * 2,
        (
            pltpu.SMEM((N_WIDE,), jnp.int32), pltpu.SMEM((N_WIDE,), jnp.int32),
            pltpu.VMEM((E_DEV, 2 * NV), BF16), pltpu.VMEM((2 * NV, NV), F32),
            pltpu.VMEM((HEAD * P_SIZE, NV), BF16), pltpu.VMEM((TAIL * P_SIZE, NV), BF16),
            pltpu.VMEM((16, P_SIZE * P_SIZE), BF16), pltpu.VMEM((BLK_TAIL, P_SIZE * P_SIZE), BF16),
            held(48 * PITCH, F32), held(2 * MESSAGE), pltpu.SemaphoreType.DMA((8,)),
        ),
    )
    other = swapped(to_other, 1)
    pair = swapped(to_pair, 0)

    own, matrices, faces = call(
        own_kernel, "own", [vmem()] * 4, (wt_own, dirs, rows_of, face_blocks),
        (slots, slots, pltpu.VMEM((P_SIZE, FACES * P_SIZE), BF16)),
        scratch=(held(16 * (P_SIZE + 1), F32),),
        flops=10**9, moved=6 * 2**20,
    )

    above, below, came, cap, wt = call(
        arrive_kernel, "arrive", [vmem()] * 2 + [smem()] + [vmem()] * 3, (other, pair, cnt, cap_own, wt_own, own),
        (layer, layer, held(2 * ARRIVED), column, column),
        scratch=(held(2 * MIG * P_SIZE), pltpu.VMEM((2 * NV, NV), F32)),
    )
    from_below = shifted(above, "narrow", -1)
    from_above = shifted(below, "narrow", 1)

    blk, partial, first, nxt = call(
        first_kernel, "first", [smem()] * 2 + [vmem()] * 11,
        (cnt, nbr, cap, wt, faces, dirs, own, matrices, came, above, below, pair, other),
        (held(E_BAL * P_SIZE), held(2 * LAYER * P_SIZE, F32), inner, inner),
        scratch=(held((ABOVE + 1) * P_SIZE), held(P_SIZE, F32)),
        flops=2 * 10**9, moved=8 * 2**20,
    )
    ends, go_other, go_pair, go_above, go_below, onward = call(
        ends_kernel, "ends", [smem()] * 2 + [vmem()] * 6, (cnt, nbr, wt, faces, partial, from_above, from_below, nxt),
        (held(2 * LAYER * P_SIZE), rim, rim, layer, layer, held(E_BAL * P_SIZE)),
        scratch=(held(2 * RIM * P_SIZE),),
    )
    other = swapped(go_other, 1)
    pair = swapped(go_pair, 0)
    came_below = shifted(go_above, "narrow", -1)
    came_above = shifted(go_below, "narrow", 1)
    result = jax.ShapeDtypeStruct((E_BAL * P_SIZE, NV), BF16)
    (inside,) = call(
        inner_kernel, "inner", [vmem()] + [smem()] * 2 + [vmem()] * 6,
        (pair, cnt, nbr, cap, faces, blk, first, ends, onward),
        (held(E_BAL * P_SIZE, F32),),
        scratch=(held((ABOVE + 1) * P_SIZE),),
        flops=10**9, moved=6 * 2**20,
    )
    (out,) = call(
        second_kernel, "second", [vmem()] + [smem()] * 2 + [vmem()] * 4,
        (other, cnt, nbr, faces, inside, came_above, came_below),
        (result,), [hbm()],
        scratch=(
            held((RIM + 1) * P_SIZE), held(E_BAL * P_SIZE), pltpu.SemaphoreType.DMA((E_BAL // PIECE,)),
        ),
        flops=10**9, moved=6 * 2**20,
    )
    return out.reshape(1, E_BAL, P_SIZE, NV)


def solution(mesh):
    in_specs = (
        P("narrow", "wide", None),
        P("narrow", "wide", None, None),
        P("narrow", "wide", None),
        P(),
        P(),
        P("narrow", None, "wide"),
        P(),
    )
    out_specs = P("narrow", "wide", None, None)
    return jax.shard_map(
        per_device, mesh=mesh, in_specs=in_specs, out_specs=out_specs, check_vma=False
    )
```
